512 devices in a mesh: dp: 8 (over y_lo, x), shard: 64 (over y_hi, z, core).
Axes of the slice: x: 4, y: 4 (y_hi: 2, y_lo: 2; y = y_hi * 2 + y_lo), z: 16, core: 2. Of those that a mesh axis runs over, the one named last changes fastest.
Arguments:
- features: bfloat16 [16, 4096, 512], P('dp', 'shard'), may hold values from -6 to 6
- upstream: bfloat16 [16, 4096, 14336], P('dp', 'shard'), may hold values from -6 to 6
- lengths: int32 [16], P('dp'), may hold values from 2048 to 4096, as said below
- weights: bfloat16 [14336, 512], P(('dp', 'shard')), may hold values from -0.25 to 0.25
Outputs:
- inv_diag: float32 [14336, 512], P(('dp', 'shard'))
- saliency: float32 [14336, 512], P(('dp', 'shard'))
- fisher_step: float32 [14336, 512], P(('dp', 'shard'))
The draws below stay inside these ranges and needn't reach their ends.
Inputs may be any that keep to these rules, and one draw needn't show every extreme that they name: `lengths`: some example has all 4096 positions valid and some exactly half of them.
All inputs are finite; a program needn't handle non-finite values.
Results may differ from the reference program's by a relative error of at most 0.002.
Values may be sent and summed in bfloat16 or wider, within the bound.
No kernel may reach another device: no remote copies, remote signals or barrier semaphores. Data moves between devices by JAX's collectives and lax.ppermute only.
A program may use at most 128 MiB of HBM per device.

```python
import jax
import jax.numpy as jnp
from jax import lax

FF = 14336
ROWS = 512
BLOCK = 128
LENGTH = 4096
EXAMPLES = 16


def draw_lengths(key, part):
    base = jax.random.randint(jax.random.fold_in(key, 11), (EXAMPLES,), LENGTH // 2, LENGTH + 1)
    order = jax.random.permutation(jax.random.fold_in(key, 23), EXAMPLES)
    places = jnp.arange(EXAMPLES)
    base = jnp.where(places == order[0], LENGTH, base)
    base = jnp.where(places == order[1], LENGTH // 2, base)
    return base.astype(jnp.int32)


def level_of(stream_key, dims, split, low, high):
    gain = 1.0
    for dim, blocks in split:
        heights = jax.random.uniform(jax.random.fold_in(jax.random.fold_in(stream_key, 6), dim), (blocks,), jnp.float32, low / len(split), high / len(split))
        gain = gain * jnp.repeat(jnp.exp(heights), dims[dim] // blocks).reshape((-1,) + (1,) * (len(dims) - 1 - dim))
    return gain


def normal_values(key, extent, scale, most, cuts=(), kind=jnp.bfloat16):
    loudness = level_of(key, extent, cuts, -0.22, 0.18) if cuts else 1.0
    values = jax.random.normal(key, extent, jnp.float32) * scale * loudness
    return jnp.minimum(jnp.maximum(values, -most), most).astype(kind)


def setup_inputs(seed: int = 0) -> dict:
    splits = jax.random.split(jax.random.key(seed), 5)
    features = normal_values(splits[0], (EXAMPLES, LENGTH, ROWS), 1.0, 6.0, ((0, 8), (1, 64)))
    upstream = normal_values(splits[1], (EXAMPLES, LENGTH, FF), 1.0, 6.0, ((0, 8), (1, 64)))
    lengths = draw_lengths(jax.random.fold_in(splits[4], 71), 0)
    weights = normal_values(splits[3], (FF, ROWS), ROWS ** -0.5, 0.25, ((0, 512),))
    return {"features": features, "upstream": upstream, "lengths": lengths, "weights": weights}


def reference(features, upstream, lengths, weights):
    positions = jnp.arange(LENGTH, dtype=jnp.int32)

    def one_example(inputs):
        feat, cotan, valid_len = inputs
        kept_rows = (positions < valid_len)[:, None]
        masked = jnp.where(kept_rows, feat, jnp.zeros_like(feat))
        product = jnp.dot(cotan.astype(jnp.float32).T.astype(jnp.float32), masked.astype(jnp.float32), preferred_element_type=jnp.float32)
        return product / valid_len.astype(jnp.float32)
    grads = lax.map(one_example, (features, upstream, lengths))
    nblocks = FF * ROWS // BLOCK
    blocks = jnp.transpose(grads.reshape(EXAMPLES, nblocks, BLOCK), (1, 0, 2))
    shift = BLOCK / LENGTH
    gram = jnp.einsum('nib,njb->nij', blocks, blocks, precision=lax.Precision.HIGHEST)
    kernel = gram + shift * jnp.eye(EXAMPLES, dtype=jnp.float32)[None]
    factor = jnp.linalg.cholesky(kernel)
    solved = jax.scipy.linalg.cho_solve((factor, True), blocks)
    diag_part = 1.0 - lax.optimization_barrier(jnp.sum(blocks * solved, axis=1))
    wblocks = weights.astype(jnp.float32).reshape(nblocks, BLOCK)
    projected = jnp.einsum('nib,nb->ni', solved, wblocks, precision=lax.Precision.HIGHEST)
    step_part = wblocks - jnp.einsum('nib,ni->nb', blocks, projected, precision=lax.Precision.HIGHEST)
    inv_diag = diag_part.reshape(FF, ROWS)
    saliency = ROWS * jnp.square(weights.astype(jnp.float32)) / (2.0 * inv_diag)
    fisher_step = jnp.sqrt(float(ROWS)) * step_part.reshape(FF, ROWS)
    return (inv_diag, saliency, fisher_step)
```

```python
import functools

import jax
import jax.numpy as jnp
from jax import lax
from jax.experimental import pallas as pl
from jax.experimental.pallas import tpu as pltpu
from jax.sharding import Mesh, PartitionSpec as P

BLOCK = 128
AXES = ("ylo", "x", "yhi", "z", "core")
NZ = 16
GROUPS = ((8, 7, 9), (6, 10, 5, 11), (4, 12, 3, 13), (2, 14, 1, 15, 0))
SWAP = [(0, 1), (1, 0)]
f32 = jnp.float32
f16 = jnp.float16


def turn_kernel(s_ref, k0, k1, r0, r1, *rest):
    outs, hold = rest[:-1], rest[-1]
    turned = []
    for k, r in ((k0, r0), (k1, r1)):
        both = jnp.concatenate([k[...].astype(f32), r[...].astype(f32)], axis=0)
        turned.append(both.T)
    span = turned[0].shape[0] // NZ
    for dest in range(NZ):
        rows = [t[dest * span:(dest + 1) * span] for t in turned]
        hold[dest] = jnp.concatenate(rows, axis=0).astype(hold.dtype)
    z, sign = s_ref[1], s_ref[2]
    for out, group in zip(outs, GROUPS):
        for i, slot in enumerate(group):
            out[i, 0] = hold[lax.rem(z + sign * slot + NZ, NZ)]


def turn(upstream, other, scalars, n_groups):
    _, seg, units = upstream.shape
    width = units // (2 * n_groups)
    span2 = 2 * width // NZ
    kept = lambda j: pl.BlockSpec((None, seg, width), lambda i, s: (s[0], 0, 2 * (2 * i + j) + s[3]))
    sent = lambda j: pl.BlockSpec((seg, width), lambda i, s: (0, 2 * (2 * i + j) + s[3]))
    grid = (n_groups // 2,)
    return pl.pallas_call(
        turn_kernel,
        grid_spec=pltpu.PrefetchScalarGridSpec(
            num_scalar_prefetch=1,
            grid=grid,
            in_specs=[kept(0), kept(1), sent(0), sent(1)],
            out_specs=[
                pl.BlockSpec((len(g), 1, span2, 2 * seg), lambda i, s: (0, i, 0, 0)) for g in GROUPS
            ],
            scratch_shapes=[pltpu.VMEM((NZ, span2, 2 * seg), upstream.dtype)],
        ),
        out_shape=[
            jax.ShapeDtypeStruct((len(g), grid[0], span2, 2 * seg), upstream.dtype) for g in GROUPS
        ],
        compiler_params=pltpu.CompilerParams(vmem_limit_bytes=40 * 1024 * 1024),
    )(scalars, upstream, upstream, other, other)


def solve_kernel(shift, scale, g_ref, w_ref, inv_ref, sal_ref, step_ref, y_ref):
    n_ex = g_ref.shape[0]
    units = w_ref.shape[0]
    rows = w_ref.shape[1]
    pad = g_ref.shape[1]
    nb = rows // BLOCK

    def blocks(x):
        return jnp.concatenate([x[:, b * BLOCK:(b + 1) * BLOCK] for b in range(nb)], axis=0).T

    for e in range(n_ex):
        y_ref[e] = blocks(g_ref[e])
    weights = w_ref[...].astype(f32)
    w = blocks(jnp.concatenate([weights, jnp.zeros((pad - units, rows), f32)], axis=0))
    lane_rows = lax.broadcasted_iota(jnp.int32, (n_ex, BLOCK), 0)
    kern = []
    for i in range(n_ex):
        gi = y_ref[i]
        row = jnp.zeros((n_ex, BLOCK), f32)
        for j in range(i, n_ex):
            dot = jnp.sum(gi * y_ref[j], axis=0, keepdims=True)
            if j == i:
                dot = dot + shift
            row = jnp.where(lane_rows == j, dot, row)
        kern.append(row)
    diag = jnp.ones((BLOCK, BLOCK), f32)
    step = w
    for k in range(n_ex):
        pivot = kern[k]
        inv = 1.0 / pivot[k:k + 1]
        yk = y_ref[k]
        scaled = yk * inv
        diag = diag - yk * scaled
        step = step - scaled * jnp.sum(yk * w, axis=0, keepdims=True)
        for i in range(k + 1, n_ex):
            m = pivot[i:i + 1] * inv
            kern[i] = kern[i] - m * pivot
            y_ref[i] = y_ref[i] - m * yk
    diag = diag.T
    step = step.T * scale
    for b in range(nb):
        at = pl.ds(b * BLOCK, BLOCK)
        d = diag[b * pad:b * pad + units]
        wb = weights[:, b * BLOCK:(b + 1) * BLOCK]
        inv_ref[:, at] = d
        sal_ref[:, at] = rows * (wb * wb) / (2.0 * d)
        step_ref[:, at] = step[b * pad:b * pad + units]


def solve(grads, weights, shift):
    units, rows = weights.shape
    out = jax.ShapeDtypeStruct((units, rows), f32)
    return pl.pallas_call(
        functools.partial(solve_kernel, shift, float(rows) ** 0.5),
        out_shape=[out, out, out],
        scratch_shapes=[pltpu.VMEM((grads.shape[0], BLOCK, BLOCK), f32)],
        compiler_params=pltpu.CompilerParams(vmem_limit_bytes=40 * 1024 * 1024),
    )(grads, weights)


def ring_pairs(direction):
    pairs = []
    for z in range(NZ):
        for core in range(2):
            step = direction if core == 0 else -direction
            pairs.append((z * 2 + core, ((z + step) % NZ) * 2 + core))
    return pairs


def body(features, upstream, lengths, weights):
    yhi, z, core = lax.axis_index("yhi"), lax.axis_index("z"), lax.axis_index("core")
    _, seg, rows = features.shape
    units = upstream.shape[2]
    n_groups = 8
    total_len = seg * 64
    shard = (yhi * NZ + z) * 2 + core
    positions = shard * seg + jnp.arange(seg, dtype=jnp.int32)
    kept_rows = positions[None, :] < lengths[:, None]
    masked = jnp.where(kept_rows[:, :, None], features, jnp.zeros_like(features)) * jnp.asarray(0.25, features.dtype)

    pick = lambda x, i: lax.dynamic_index_in_dim(x, i, 0, keepdims=False)
    other = lax.ppermute(pick(upstream, 1 - core), "core", SWAP)
    mine = jnp.concatenate([pick(masked, core), lax.ppermute(pick(masked, 1 - core), "core", SWAP)], axis=0)
    theirs = lax.ppermute(mine, "yhi", SWAP)

    sign = 1 - 2 * core
    scalars = lambda half: jnp.stack([core, z, sign, half]).astype(jnp.int32)
    away = turn(upstream, other, scalars(1 - yhi), n_groups)
    arrived = [lax.ppermute(a, "yhi", SWAP) for a in away]
    home = turn(upstream, other, scalars(yhi), n_groups)

    parts = {}
    chunk = units // 2 // NZ
    for group, a, b in zip(GROUPS, home, arrived):
        dims = (((1,), (0,)), ((), ()))
        flat = lambda x: x.reshape(-1, x.shape[-1])
        part = lax.dot_general(flat(a), mine, dims, preferred_element_type=f32)
        part = part + lax.dot_general(flat(b), theirs, dims, preferred_element_type=f32)
        for i, slot in enumerate(group):
            parts[slot] = part[i * chunk:(i + 1) * chunk]

    half = chunk // 2
    pairs = (ring_pairs(1), ring_pairs(-1))
    slot_of = (lambda d: d, lambda d: NZ - d)
    sums = [parts[8][:half].astype(f16), parts[8][half:].astype(f16)]
    for dist in range(7, -1, -1):
        for k in range(2):
            got = lax.ppermute(sums[k], ("z", "core"), pairs[k])
            if dist == 0:
                sums[k] = got
                continue
            if dist == 7:
                empty = jnp.zeros_like(got)
                got = jnp.concatenate([got, empty] if k == 0 else [empty, got], axis=0)
            sums[k] = (got.astype(f32) + parts[slot_of[k](dist)]).astype(f16)
        if dist:
            sums = list(lax.optimization_barrier(tuple(sums)))
    length = pick(lengths, core).astype(f32)
    total = (sums[0].astype(f32) + sums[1].astype(f32) + parts[0]) * (4096.0 / length)
    pieces = total.astype(f16).reshape(2 * n_groups, -1, rows)
    owned = lax.all_to_all(pieces, ("ylo", "x", "core"), 0, 0, tiled=True)
    own_units = owned.shape[1]
    grads = owned.astype(f32) * (1.0 / 1024.0)
    grads = jnp.pad(grads, ((0, 0), (0, -own_units % 8), (0, 0)))
    return tuple(solve(grads, weights, BLOCK / total_len))


def solution(mesh):
    fine = Mesh(mesh.devices.reshape(2, 4, 2, NZ, 2), AXES)
    dp, shard = ("ylo", "x"), ("yhi", "z", "core")
    in_specs = (P(dp, shard, None), P(dp, shard, None), P(dp), P(dp + shard, None))
    out_specs = (P(dp + shard, None),) * 3
    return jax.shard_map(body, mesh=fine, in_specs=in_specs, out_specs=out_specs, check_vma=False)
```

```python
import functools

import jax
import jax.numpy as jnp
from jax import lax
from jax.experimental import pallas as pl
from jax.experimental.pallas import tpu as pltpu
from jax.sharding import Mesh, PartitionSpec as P

BLOCK = 128
AXES = ("ylo", "x", "yhi", "z", "core")
NZ = 16
GROUPS = ((8, 7, 9), (6, 10, 5, 11), (4, 12, 3, 13), (2, 14, 1, 15, 0))
SWAP = [(0, 1), (1, 0)]
f32 = jnp.float32
f16 = jnp.float16


def turn_kernel(s_ref, k0, k1, r0, r1, *rest):
    outs, hold = rest[:-1], rest[-1]
    turned = []
    for k, r in ((k0, r0), (k1, r1)):
        both = jnp.concatenate([k[...].astype(f32), r[...].astype(f32)], axis=0)
        turned.append(both.T)
    span = turned[0].shape[0] // NZ
    for dest in range(NZ):
        rows = [t[dest * span:(dest + 1) * span] for t in turned]
        hold[dest] = jnp.concatenate(rows, axis=0).astype(hold.dtype)
    z, sign = s_ref[1], s_ref[2]
    for out, group in zip(outs, GROUPS):
        for i, slot in enumerate(group):
            out[i, 0] = hold[lax.rem(z + sign * slot + NZ, NZ)]


def turn(upstream, other, scalars, n_groups):
    _, seg, units = upstream.shape
    width = units // (2 * n_groups)
    span2 = 2 * width // NZ
    kept = lambda j: pl.BlockSpec((None, seg, width), lambda i, s: (s[0], 0, 2 * (2 * i + j) + s[3]))
    sent = lambda j: pl.BlockSpec((seg, width), lambda i, s: (0, 2 * (2 * i + j) + s[3]))
    grid = (n_groups // 2,)
    return pl.pallas_call(
        turn_kernel,
        grid_spec=pltpu.PrefetchScalarGridSpec(
            num_scalar_prefetch=1,
            grid=grid,
            in_specs=[kept(0), kept(1), sent(0), sent(1)],
            out_specs=[
                pl.BlockSpec((len(g), 1, span2, 2 * seg), lambda i, s: (0, i, 0, 0)) for g in GROUPS
            ],
            scratch_shapes=[pltpu.VMEM((NZ, span2, 2 * seg), upstream.dtype)],
        ),
        out_shape=[
            jax.ShapeDtypeStruct((len(g), grid[0], span2, 2 * seg), upstream.dtype) for g in GROUPS
        ],
        compiler_params=pltpu.CompilerParams(vmem_limit_bytes=40 * 1024 * 1024),
    )(scalars, upstream, upstream, other, other)


def solve_kernel(shift, scale, g_ref, w_ref, inv_ref, sal_ref, step_ref, y_ref):
    n_ex = g_ref.shape[0]
    units = w_ref.shape[0]
    rows = w_ref.shape[1]
    pad = g_ref.shape[1]
    nb = rows // BLOCK

    def blocks(x):
        return jnp.concatenate([x[:, b * BLOCK:(b + 1) * BLOCK] for b in range(nb)], axis=0).T

    for e in range(n_ex):
        y_ref[e] = blocks(g_ref[e])
    weights = w_ref[...].astype(f32)
    w = blocks(jnp.concatenate([weights, jnp.zeros((pad - units, rows), f32)], axis=0))
    lane_rows = lax.broadcasted_iota(jnp.int32, (n_ex, BLOCK), 0)
    kern = []
    for i in range(n_ex):
        gi = y_ref[i]
        row = jnp.zeros((n_ex, BLOCK), f32)
        for j in range(i, n_ex):
            dot = jnp.sum(gi * y_ref[j], axis=0, keepdims=True)
            if j == i:
                dot = dot + shift
            row = jnp.where(lane_rows == j, dot, row)
        kern.append(row)
    diag = jnp.ones((BLOCK, BLOCK), f32)
    step = w
    for k in range(n_ex):
        pivot = kern[k]
        inv = 1.0 / pivot[k:k + 1]
        yk = y_ref[k]
        scaled = yk * inv
        diag = diag - yk * scaled
        step = step - scaled * jnp.sum(yk * w, axis=0, keepdims=True)
        for i in range(k + 1, n_ex):
            m = pivot[i:i + 1] * inv
            kern[i] = kern[i] - m * pivot
            y_ref[i] = y_ref[i] - m * yk
    diag = diag.T
    step = step.T * scale
    for b in range(nb):
        at = pl.ds(b * BLOCK, BLOCK)
        d = diag[b * pad:b * pad + units]
        wb = weights[:, b * BLOCK:(b + 1) * BLOCK]
        inv_ref[:, at] = d
        sal_ref[:, at] = rows * (wb * wb) / (2.0 * d)
        step_ref[:, at] = step[b * pad:b * pad + units]


def solve(grads, weights, shift):
    units, rows = weights.shape
    out = jax.ShapeDtypeStruct((units, rows), f32)
    return pl.pallas_call(
        functools.partial(solve_kernel, shift, float(rows) ** 0.5),
        out_shape=[out, out, out],
        scratch_shapes=[pltpu.VMEM((grads.shape[0], BLOCK, BLOCK), f32)],
        compiler_params=pltpu.CompilerParams(vmem_limit_bytes=40 * 1024 * 1024),
    )(grads, weights)


def ring_pairs(direction):
    pairs = []
    for z in range(NZ):
        for core in range(2):
            step = direction if core == 0 else -direction
            pairs.append((z * 2 + core, ((z + step) % NZ) * 2 + core))
    return pairs


def body(features, upstream, lengths, weights):
    yhi, z, core = lax.axis_index("yhi"), lax.axis_index("z"), lax.axis_index("core")
    _, seg, rows = features.shape
    units = upstream.shape[2]
    n_groups = 8
    total_len = seg * 64
    shard = (yhi * NZ + z) * 2 + core
    positions = shard * seg + jnp.arange(seg, dtype=jnp.int32)
    kept_rows = positions[None, :] < lengths[:, None]
    masked = jnp.where(kept_rows[:, :, None], features, jnp.zeros_like(features)) * jnp.asarray(0.25, features.dtype)

    pick = lambda x, i: lax.dynamic_index_in_dim(x, i, 0, keepdims=False)
    other = lax.ppermute(pick(upstream, 1 - core), "core", SWAP)
    mine, rest = pick(masked, core), pick(masked, 1 - core)
    theirs = jnp.concatenate([
        lax.ppermute(mine, "yhi", SWAP),
        lax.ppermute(rest, ("yhi", "core"), [(i, 3 - i) for i in range(4)]),
    ], axis=0)
    mine = jnp.concatenate([mine, lax.ppermute(rest, "core", SWAP)], axis=0)

    sign = 1 - 2 * core
    scalars = lambda half: jnp.stack([core, z, sign, half]).astype(jnp.int32)
    away = turn(upstream, other, scalars(1 - yhi), n_groups)
    arrived = [lax.ppermute(a, "yhi", SWAP) for a in away]
    home = turn(upstream, other, scalars(yhi), n_groups)

    parts = {}
    chunk = units // 2 // NZ
    for group, a, b in zip(GROUPS, home, arrived):
        dims = (((1,), (0,)), ((), ()))
        flat = lambda x: x.reshape(-1, x.shape[-1])
        part = lax.dot_general(flat(a), mine, dims, preferred_element_type=f32)
        part = part + lax.dot_general(flat(b), theirs, dims, preferred_element_type=f32)
        for i, slot in enumerate(group):
            parts[slot] = part[i * chunk:(i + 1) * chunk]

    half = chunk // 2
    pairs = (ring_pairs(1), ring_pairs(-1))
    slot_of = (lambda d: d, lambda d: NZ - d)
    sums = [parts[8][:half].astype(f16), parts[8][half:].astype(f16)]
    last = None
    for dist in range(7, -1, -1):
        for k in range(2):
            got = lax.ppermute(sums[k], ("z", "core"), pairs[k])
            if dist == 0:
                sums[k] = got
                continue
            if last is not None:
                got, _ = lax.optimization_barrier((got, last))
            if dist == 7:
                empty = jnp.zeros_like(got)
                got = jnp.concatenate([got, empty] if k == 0 else [empty, got], axis=0)
            sums[k] = last = (got.astype(f32) + parts[slot_of[k](dist)]).astype(f16)
    length = pick(lengths, core).astype(f32)
    total = (sums[0].astype(f32) + sums[1].astype(f32) + parts[0]) * (4096.0 / length)
    pieces = total.astype(f16).reshape(2 * n_groups, -1, rows)
    owned = lax.all_to_all(pieces, ("ylo", "x", "core"), 0, 0, tiled=True)
    own_units = owned.shape[1]
    grads = owned.astype(f32) * (1.0 / 1024.0)
    grads = jnp.pad(grads, ((0, 0), (0, -own_units % 8), (0, 0)))
    return tuple(solve(grads, weights, BLOCK / total_len))


def solution(mesh):
    fine = Mesh(mesh.devices.reshape(2, 4, 2, NZ, 2), AXES)
    dp, shard = ("ylo", "x"), ("yhi", "z", "core")
    in_specs = (P(dp, shard, None), P(dp, shard, None), P(dp), P(dp + shard, None))
    out_specs = (P(dp + shard, None),) * 3
    return jax.shard_map(body, mesh=fine, in_specs=in_specs, out_specs=out_specs, check_vma=False)
```

```python
import functools

import jax
import jax.numpy as jnp
from jax import lax
from jax.experimental import pallas as pl
from jax.experimental.pallas import tpu as pltpu
from jax.sharding import Mesh, PartitionSpec as P

BLOCK = 128
AXES = ("ylo", "x", "yhi", "z", "core")
NZ = 16
FAR = NZ // 2
VMEM = 56 * 1024 * 1024
f32 = jnp.float32
f16 = jnp.float16


def turn_kernel(s_ref, up_ref, feat_ref, *rest):
    outs, hold = rest[:-1], rest[-1]
    step = pl.program_id(0)
    seg2, width = feat_ref.shape[0], up_ref.shape[2] // 4
    span = width // NZ
    for half in range(2):
        turned = []
        for j in range(2):
            x = up_ref[:, :, (2 * j + half) * width:(2 * j + half + 1) * width]
            turned.append(x.reshape(seg2, width).astype(f32).T)
        for dest in range(NZ):
            rows = [t[dest * span:(dest + 1) * span] for t in turned]
            hold[half, dest, step] = jnp.concatenate(rows, axis=0).astype(hold.dtype)

    @pl.when(step == pl.num_programs(0) - 1)
    def _():
        n, tall = hold.shape[2], hold.shape[3]
        yhi, z, core = s_ref[0], s_ref[1], s_ref[2]
        for other in range(4):
            half = yhi if other < 2 else 1 - yhi
            to = core if other % 2 == 0 else 1 - core
            first, second = outs[2 * other], outs[2 * other + 1]
            place = lambda dist: lax.rem(z + (1 - 2 * to) * dist + NZ, NZ)
            for p in range(n // 2):
                first[p * tall:(p + 1) * tall] = hold[half, place(FAR), (n // 2) * to + p]
            for p in range(n):
                at = (n // 2 + p) * tall
                first[at:at + tall] = hold[half, place(FAR - 1), p]
            at = (n // 2 + n) * tall
            for b in range(feat_ref.shape[1] // BLOCK):
                first[at + b * seg2:at + (b + 1) * seg2] = feat_ref[:, b * BLOCK:(b + 1) * BLOCK]
            for i in range(FAR - 1):
                for p in range(n):
                    at = (i * n + p) * tall
                    second[at:at + tall] = hold[half, place(FAR - 2 - i), p]


def turn(upstream, feats, scalars, n_groups):
    _, seg, units = upstream.shape
    seg2, rows = feats.shape
    n = n_groups // 2
    chunk = units // 2 // NZ
    tall = chunk // n
    shapes = [(chunk // 2 + chunk + rows // BLOCK * seg2, seg2), ((FAR - 1) * chunk, seg2)] * 4
    whole = lambda shape: pl.BlockSpec(shape, lambda i, s: (0,) * len(shape))
    return pl.pallas_call(
        turn_kernel,
        grid_spec=pltpu.PrefetchScalarGridSpec(
            num_scalar_prefetch=1,
            grid=(n,),
            in_specs=[pl.BlockSpec((2, seg, units // n), lambda i, s: (0, 0, i)), whole(feats.shape)],
            out_specs=[whole(shape) for shape in shapes],
            scratch_shapes=[pltpu.VMEM((2, NZ, n, tall, seg2), upstream.dtype)],
        ),
        out_shape=[jax.ShapeDtypeStruct(shape, upstream.dtype) for shape in shapes],
        compiler_params=pltpu.CompilerParams(vmem_limit_bytes=VMEM),
    )(scalars, upstream, feats)


def first_kernel(a_ref, b_ref, c_ref, d_ref, out_ref, right_ref):
    refs = (a_ref, b_ref, c_ref, d_ref)
    seg2 = a_ref.shape[1]
    height = out_ref.shape[0]
    n_lane = (a_ref.shape[0] - height) // seg2
    for k, ref in enumerate(refs):
        rows = [ref[height + b * seg2:height + (b + 1) * seg2] for b in range(n_lane)]
        feats = jnp.concatenate(rows, axis=1)
        half = seg2 // 2
        none = jnp.zeros((half, feats.shape[1]), feats.dtype)
        right_ref[k * seg2:k * seg2 + half] = jnp.concatenate([feats[:half], none], axis=1)
        right_ref[k * seg2 + half:(k + 1) * seg2] = jnp.concatenate([none, feats[half:]], axis=1)
    tile = height // 3

    @pl.loop(0, 3)
    def _(i):
        at = pl.ds(pl.multiple_of(i * tile, tile), tile)
        left = jnp.concatenate([ref[at] for ref in refs], axis=1)
        out_ref[at] = jnp.dot(left, right_ref[...], preferred_element_type=f32)


def first_product(pieces, height):
    seg2 = pieces[0].shape[1]
    wide = (pieces[0].shape[0] - height) // seg2 * BLOCK * 2
    return pl.pallas_call(
        first_kernel,
        out_shape=[
            jax.ShapeDtypeStruct((height, wide), f32),
            jax.ShapeDtypeStruct((4 * seg2, wide), pieces[0].dtype),
        ],
        cost_estimate=pl.CostEstimate(flops=2 * height * 4 * seg2 * wide, bytes_accessed=6 * height * wide, transcendentals=0),
        compiler_params=pltpu.CompilerParams(vmem_limit_bytes=40 * 1024 * 1024),
    )(*pieces)


def product_kernel(a_ref, b_ref, c_ref, d_ref, right_ref, out_ref):
    left = jnp.concatenate([ref[...] for ref in (a_ref, b_ref, c_ref, d_ref)], axis=1)
    out_ref[...] = jnp.dot(left, right_ref[...], preferred_element_type=f32)


def product(pieces, right, chunk, start, count):
    seg2 = pieces[0].shape[1]
    tile = chunk // 2
    wide = right.shape[1]
    return pl.pallas_call(
        product_kernel,
        grid=(2 * count,),
        in_specs=[pl.BlockSpec((tile, seg2), lambda i: (2 * start + i, 0))] * 4
        + [pl.BlockSpec(right.shape, lambda i: (0, 0))],
        out_specs=pl.BlockSpec((tile, wide), lambda i: (i, 0)),
        out_shape=jax.ShapeDtypeStruct((count * chunk, wide), f32),
        cost_estimate=pl.CostEstimate(
            flops=2 * count * chunk * 4 * seg2 * wide, bytes_accessed=6 * count * chunk * wide, transcendentals=0
        ),
        compiler_params=pltpu.CompilerParams(vmem_limit_bytes=40 * 1024 * 1024),
    )(*pieces, right)


def solve_kernel(shift, scale, g_ref, w_ref, inv_ref, sal_ref, step_ref, y_ref):
    n_ex = g_ref.shape[0]
    units = w_ref.shape[0]
    rows = w_ref.shape[1]
    pad = g_ref.shape[1]
    nb = rows // BLOCK

    def blocks(x):
        return jnp.concatenate([x[:, b * BLOCK:(b + 1) * BLOCK] for b in range(nb)], axis=0).T

    for e in range(n_ex):
        y_ref[e] = blocks(g_ref[e])
    weights = w_ref[...].astype(f32)
    w = blocks(jnp.concatenate([weights, jnp.zeros((pad - units, rows), f32)], axis=0))
    lane_rows = lax.broadcasted_iota(jnp.int32, (n_ex, BLOCK), 0)
    kern = []
    for i in range(n_ex):
        gi = y_ref[i]
        row = jnp.zeros((n_ex, BLOCK), f32)
        for j in range(i, n_ex):
            dot = jnp.sum(gi * y_ref[j], axis=0, keepdims=True)
            if j == i:
                dot = dot + shift
            row = jnp.where(lane_rows == j, dot, row)
        kern.append(row)
    diag = jnp.ones((BLOCK, BLOCK), f32)
    step = w
    for k in range(n_ex):
        pivot = kern[k]
        inv = 1.0 / pivot[k:k + 1]
        yk = y_ref[k]
        scaled = yk * inv
        diag = diag - yk * scaled
        step = step - scaled * jnp.sum(yk * w, axis=0, keepdims=True)
        for i in range(k + 1, n_ex):
            m = pivot[i:i + 1] * inv
            kern[i] = kern[i] - m * pivot
            y_ref[i] = y_ref[i] - m * yk
    diag = diag.T
    step = step.T * scale
    for b in range(nb):
        at = pl.ds(b * BLOCK, BLOCK)
        d = diag[b * pad:b * pad + units]
        wb = weights[:, b * BLOCK:(b + 1) * BLOCK]
        inv_ref[:, at] = d
        sal_ref[:, at] = rows * (wb * wb) / (2.0 * d)
        step_ref[:, at] = step[b * pad:b * pad + units]


def solve(grads, weights, shift):
    units, rows = weights.shape
    out = jax.ShapeDtypeStruct((units, rows), f32)
    return pl.pallas_call(
        functools.partial(solve_kernel, shift, float(rows) ** 0.5),
        out_shape=[out, out, out],
        scratch_shapes=[pltpu.VMEM((grads.shape[0], BLOCK, BLOCK), f32)],
        compiler_params=pltpu.CompilerParams(vmem_limit_bytes=40 * 1024 * 1024),
    )(grads, weights)


def ring_pairs(cross):
    pairs = []
    for z in range(NZ):
        for core in range(2):
            to = (z + 1 - 2 * core) % NZ
            pairs.append((z * 2 + core, to * 2 + (core ^ cross)))
    return pairs


def body(features, upstream, lengths, weights):
    yhi, z, core = lax.axis_index("yhi"), lax.axis_index("z"), lax.axis_index("core")
    n_ex, seg, rows = features.shape
    units = upstream.shape[2]
    n_groups = 8
    total_len = seg * 64
    shard = (yhi * NZ + z) * 2 + core
    positions = shard * seg + jnp.arange(seg, dtype=jnp.int32)
    kept_rows = positions[None, :] < lengths[:, None]
    masked = jnp.where(kept_rows[:, :, None], features, jnp.zeros_like(features)) * jnp.asarray(0.25, features.dtype)
    scalars = jnp.stack([yhi, z, core]).astype(jnp.int32)
    made = turn(upstream, masked.reshape(n_ex * seg, rows), scalars, n_groups)

    quad = lambda x, i: lax.ppermute(x, ("yhi", "core"), [(j, j ^ i) for j in range(4)])
    chunk = units // 2 // NZ
    half = chunk // 2
    order = (3, 2, 1)
    near = {i: quad(made[2 * i], i) for i in order}
    rest = {i: quad(made[2 * i + 1], i) for i in order}
    near, rest = [made[0]] + [near[i] for i in (1, 2, 3)], [made[1]] + [rest[i] for i in (1, 2, 3)]
    part, right = first_product(near, half + chunk)
    parts = {FAR: part[:half], FAR - 1: part[half:]}
    start = 0
    for count in (2, FAR - 3):
        part = product(rest, right, chunk, start, count)
        for i in range(count):
            parts[FAR - 2 - start - i] = part[i * chunk:(i + 1) * chunk]
        start += count

    ring = lambda x, cross=0: lax.ppermute(x, ("z", "core"), ring_pairs(cross))
    got = ring(parts[FAR].astype(f16)).astype(f32)
    sums = [
        (parts[FAR - 1][k * half:(k + 1) * half] + jnp.where(core == k, got, 0.0)).astype(f16) for k in range(2)
    ]
    last = sums[1]
    for dist in range(FAR - 2, 0, -1):
        for k in range(2):
            got = ring(sums[k])
            got, _ = lax.optimization_barrier((got, last))
            sums[k] = last = (got.astype(f32) + parts[dist][k * half:(k + 1) * half]).astype(f16)
    pick = lambda x, i: lax.dynamic_slice_in_dim(x, i * rows, rows, 1)
    ends = []
    for k in range(2):
        ends.append(ring(pick(sums[k], core)).astype(f32) + ring(pick(sums[k], 1 - core), 1).astype(f32))
    length = lax.dynamic_index_in_dim(lengths, core, 0, keepdims=False).astype(f32)
    total = (jnp.concatenate(ends, axis=0) + pick(parts[0], core)) * (4096.0 / length)
    pieces = total.astype(f16).reshape(2 * n_groups, -1, rows)
    owned = lax.all_to_all(pieces, ("ylo", "x", "core"), 0, 0, tiled=True)
    own_units = owned.shape[1]
    grads = owned.astype(f32) * (1.0 / 1024.0)
    grads = jnp.pad(grads, ((0, 0), (0, -own_units % 8), (0, 0)))
    return tuple(solve(grads, weights, BLOCK / total_len))


def solution(mesh):
    fine = Mesh(mesh.devices.reshape(2, 4, 2, NZ, 2), AXES)
    dp, shard = ("ylo", "x"), ("yhi", "z", "core")
    in_specs = (P(dp, shard, None), P(dp, shard, None), P(dp), P(dp + shard, None))
    out_specs = (P(dp + shard, None),) * 3
    return jax.shard_map(body, mesh=fine, in_specs=in_specs, out_specs=out_specs, check_vma=False)
```

```python
import functools

import jax
import jax.numpy as jnp
from jax import lax
from jax.experimental import pallas as pl
from jax.experimental.pallas import tpu as pltpu
from jax.sharding import Mesh, PartitionSpec as P

BLOCK = 128
AXES = ("ylo", "x", "yhi", "z", "core")
NZ = 16
FAR = NZ // 2
GROUPS = ((7, 6), (5, 4), (3, 2, 1, 0))
VMEM = 56 * 1024 * 1024
f32 = jnp.float32
f16 = jnp.float16


def outputs_of(other):
    return (sum(GROUPS, ()),) if other == 1 else GROUPS


def turn_kernel(s_ref, up_ref, feat_ref, *rest):
    outs, hold = list(rest[:-1]), rest[-1]
    step = pl.program_id(0)
    n_ex, seg, n_row = feat_ref.shape
    seg2, width = n_ex * seg, up_ref.shape[2] // 4
    span = width // NZ
    for half in range(2):
        turned = []
        for j in range(2):
            x = up_ref[:, :, (2 * j + half) * width:(2 * j + half + 1) * width]
            turned.append(x.reshape(seg2, width).astype(f32).T)
        for dest in range(NZ):
            rows = [t[dest * span:(dest + 1) * span] for t in turned]
            hold[half, dest, step] = jnp.concatenate(rows, axis=0).astype(hold.dtype)

    @pl.when(step == pl.num_programs(0) - 1)
    def _():
        n, tall = hold.shape[2], hold.shape[3]
        yhi, z, core = s_ref[0], s_ref[1], s_ref[2]
        position = s_ref[3] + lax.broadcasted_iota(jnp.int32, (seg, n_row), 0)
        feats = jnp.concatenate([
            jnp.where(position < s_ref[4 + e], feat_ref[e].astype(f32) * 0.25, 0.0) for e in range(n_ex)
        ], axis=0).astype(feat_ref.dtype)
        for other in range(4):
            half = yhi if other < 2 else 1 - yhi
            to = core if other % 2 == 0 else 1 - core
            place = lambda dist: lax.rem(z + (1 - 2 * to) * dist + NZ, NZ)
            first = outs.pop(0)
            for p in range(n // 2):
                first[p * tall:(p + 1) * tall] = hold[half, place(FAR), (n // 2) * to + p]
            at = n // 2 * tall
            for b in range(n_row // BLOCK):
                first[at + b * seg2:at + (b + 1) * seg2] = feats[:, b * BLOCK:(b + 1) * BLOCK]
            for group in outputs_of(other):
                out = outs.pop(0)
                for i, dist in enumerate(group):
                    for p in range(n):
                        at = (i * n + p) * tall
                        out[at:at + tall] = hold[half, place(dist), p]


def turn(upstream, features, scalars, n_groups):
    n_ex, seg, units = upstream.shape
    rows = features.shape[2]
    seg2 = n_ex * seg
    n = n_groups // 2
    chunk = units // 2 // NZ
    shapes = []
    for other in range(4):
        shapes.append((chunk // 2 + rows // BLOCK * seg2, seg2))
        shapes += [(len(group) * chunk, seg2) for group in outputs_of(other)]
    whole = lambda shape: pl.BlockSpec(shape, lambda i, s: (0,) * len(shape))
    made = pl.pallas_call(
        turn_kernel,
        grid_spec=pltpu.PrefetchScalarGridSpec(
            num_scalar_prefetch=1,
            grid=(n,),
            in_specs=[pl.BlockSpec((n_ex, seg, units // n), lambda i, s: (0, 0, i)), whole(features.shape)],
            out_specs=[whole(shape) for shape in shapes],
            scratch_shapes=[pltpu.VMEM((2, NZ, n, chunk // n, seg2), upstream.dtype)],
        ),
        out_shape=[jax.ShapeDtypeStruct(shape, upstream.dtype) for shape in shapes],
        compiler_params=pltpu.CompilerParams(vmem_limit_bytes=VMEM),
    )(scalars, upstream, features)
    made = list(made)
    return [[made.pop(0) for _ in range(1 + len(outputs_of(other)))] for other in range(4)]


def first_kernel(a_ref, b_ref, c_ref, d_ref, out_ref, right_ref):
    refs = (a_ref, b_ref, c_ref, d_ref)
    seg2 = a_ref.shape[1]
    height = out_ref.shape[0]
    n_lane = (a_ref.shape[0] - height) // seg2
    for k, ref in enumerate(refs):
        rows = [ref[height + b * seg2:height + (b + 1) * seg2] for b in range(n_lane)]
        feats = jnp.concatenate(rows, axis=1)
        half = seg2 // 2
        none = jnp.zeros((half, feats.shape[1]), feats.dtype)
        right_ref[k * seg2:k * seg2 + half] = jnp.concatenate([feats[:half], none], axis=1)
        right_ref[k * seg2 + half:(k + 1) * seg2] = jnp.concatenate([none, feats[half:]], axis=1)
    left = jnp.concatenate([ref[:height] for ref in refs], axis=1)
    out_ref[...] = jnp.dot(left, right_ref[...], preferred_element_type=f32)


def first_product(pieces, height):
    seg2 = pieces[0].shape[1]
    wide = (pieces[0].shape[0] - height) // seg2 * BLOCK * 2
    return pl.pallas_call(
        first_kernel,
        out_shape=[
            jax.ShapeDtypeStruct((height, wide), f32),
            jax.ShapeDtypeStruct((4 * seg2, wide), pieces[0].dtype),
        ],
        cost_estimate=pl.CostEstimate(flops=200 * height * 4 * seg2 * wide, bytes_accessed=6 * height * wide, transcendentals=0),
        compiler_params=pltpu.CompilerParams(vmem_limit_bytes=40 * 1024 * 1024),
    )(*pieces)


def product_kernel(a_ref, b_ref, c_ref, d_ref, right_ref, out_ref):
    left = jnp.concatenate([ref[...] for ref in (a_ref, b_ref, c_ref, d_ref)], axis=1)
    out_ref[...] = jnp.dot(left, right_ref[...], preferred_element_type=f32)


def product(pieces, starts, right, chunk, count):
    seg2 = pieces[0].shape[1]
    tile = chunk // 2
    wide = right.shape[1]
    return pl.pallas_call(
        product_kernel,
        grid=(2 * count,),
        in_specs=[pl.BlockSpec((tile, seg2), lambda i, start=start: (2 * start + i, 0)) for start in starts]
        + [pl.BlockSpec(right.shape, lambda i: (0, 0))],
        out_specs=pl.BlockSpec((tile, wide), lambda i: (i, 0)),
        out_shape=jax.ShapeDtypeStruct((count * chunk, wide), f32),
        cost_estimate=pl.CostEstimate(
            flops=80 * count * chunk * 4 * seg2 * wide, bytes_accessed=6 * count * chunk * wide, transcendentals=0
        ),
        compiler_params=pltpu.CompilerParams(vmem_limit_bytes=40 * 1024 * 1024),
    )(*pieces, right)


def solve_kernel(shift, scale, g_ref, w_ref, inv_ref, sal_ref, step_ref, y_ref):
    n_ex = g_ref.shape[0]
    units = w_ref.shape[0]
    rows = w_ref.shape[1]
    pad = g_ref.shape[1]
    nb = rows // BLOCK

    def blocks(x):
        return jnp.concatenate([x[:, b * BLOCK:(b + 1) * BLOCK] for b in range(nb)], axis=0).T

    for e in range(n_ex):
        y_ref[e] = blocks(g_ref[e])
    weights = w_ref[...].astype(f32)
    w = blocks(jnp.concatenate([weights, jnp.zeros((pad - units, rows), f32)], axis=0))
    lane_rows = lax.broadcasted_iota(jnp.int32, (n_ex, BLOCK), 0)
    kern = []
    for i in range(n_ex):
        gi = y_ref[i]
        row = jnp.zeros((n_ex, BLOCK), f32)
        for j in range(i, n_ex):
            dot = jnp.sum(gi * y_ref[j], axis=0, keepdims=True)
            if j == i:
                dot = dot + shift
            row = jnp.where(lane_rows == j, dot, row)
        kern.append(row)
    diag = jnp.ones((BLOCK, BLOCK), f32)
    step = w
    for k in range(n_ex):
        pivot = kern[k]
        inv = 1.0 / pivot[k:k + 1]
        yk = y_ref[k]
        scaled = yk * inv
        diag = diag - yk * scaled
        step = step - scaled * jnp.sum(yk * w, axis=0, keepdims=True)
        for i in range(k + 1, n_ex):
            m = pivot[i:i + 1] * inv
            kern[i] = kern[i] - m * pivot
            y_ref[i] = y_ref[i] - m * yk
    diag = diag.T
    step = step.T * scale
    for b in range(nb):
        at = pl.ds(b * BLOCK, BLOCK)
        d = diag[b * pad:b * pad + units]
        wb = weights[:, b * BLOCK:(b + 1) * BLOCK]
        inv_ref[:, at] = d
        sal_ref[:, at] = rows * (wb * wb) / (2.0 * d)
        step_ref[:, at] = step[b * pad:b * pad + units]


def solve(grads, weights, shift):
    units, rows = weights.shape
    out = jax.ShapeDtypeStruct((units, rows), f32)
    return pl.pallas_call(
        functools.partial(solve_kernel, shift, float(rows) ** 0.5),
        out_shape=[out, out, out],
        scratch_shapes=[pltpu.VMEM((grads.shape[0], BLOCK, BLOCK), f32)],
        compiler_params=pltpu.CompilerParams(vmem_limit_bytes=40 * 1024 * 1024),
    )(grads, weights)


def ring_pairs(cross):
    pairs = []
    for z in range(NZ):
        for core in range(2):
            to = (z + 1 - 2 * core) % NZ
            pairs.append((z * 2 + core, to * 2 + (core ^ cross)))
    return pairs


def body(features, upstream, lengths, weights):
    yhi, z, core = lax.axis_index("yhi"), lax.axis_index("z"), lax.axis_index("core")
    n_ex, seg, rows = features.shape
    units = upstream.shape[2]
    n_groups = 8
    total_len = seg * 64
    shard = (yhi * NZ + z) * 2 + core
    scalars = jnp.concatenate([jnp.stack([yhi, z, core, shard * seg]), lengths]).astype(jnp.int32)
    made = turn(upstream, features, scalars, n_groups)

    quad = lambda x, i: lax.ppermute(x, ("yhi", "core"), [(j, j ^ i) for j in range(4)])
    chunk = units // 2 // NZ
    half = chunk // 2
    got = {i: [quad(x, i) for x in made[i]] for i in (2, 3, 1)}
    got[0] = made[0]
    far, right = first_product([got[i][0] for i in range(4)], half)
    parts = {}
    start = 0
    for g, group in enumerate(GROUPS):
        pieces = [got[0][1 + g], got[1][1], got[2][1 + g], got[3][1 + g]]
        part = product(pieces, (0, start, 0, 0), right, chunk, len(group))
        for i, dist in enumerate(group):
            parts[dist] = part[i * chunk:(i + 1) * chunk]
        start += len(group)

    ring = lambda x, cross=0: lax.ppermute(x, ("z", "core"), ring_pairs(cross))
    got = ring(far.astype(f16)).astype(f32)
    sums = [
        (parts[FAR - 1][k * half:(k + 1) * half] + jnp.where(core == k, got, 0.0)).astype(f16) for k in range(2)
    ]
    last = sums[1]
    for dist in range(FAR - 2, 0, -1):
        for k in range(2):
            got = ring(sums[k])
            got, _ = lax.optimization_barrier((got, last))
            sums[k] = last = (got.astype(f32) + parts[dist][k * half:(k + 1) * half]).astype(f16)
    pick = lambda x, i: lax.dynamic_slice_in_dim(x, i * rows, rows, 1)
    ends = []
    for k in range(2):
        ends.append(ring(pick(sums[k], core)).astype(f32) + ring(pick(sums[k], 1 - core), 1).astype(f32))
    length = lax.dynamic_index_in_dim(lengths, core, 0, keepdims=False).astype(f32)
    total = (jnp.concatenate(ends, axis=0) + pick(parts[0], core)) * (4096.0 / length)
    pieces = total.astype(f16).reshape(2 * n_groups, -1, rows)
    owned = lax.all_to_all(pieces, ("ylo", "x", "core"), 0, 0, tiled=True)
    own_units = owned.shape[1]
    grads = owned.astype(f32) * (1.0 / 1024.0)
    grads = jnp.pad(grads, ((0, 0), (0, -own_units % 8), (0, 0)))
    return tuple(solve(grads, weights, BLOCK / total_len))


def solution(mesh):
    fine = Mesh(mesh.devices.reshape(2, 4, 2, NZ, 2), AXES)
    dp, shard = ("ylo", "x"), ("yhi", "z", "core")
    in_specs = (P(dp, shard, None), P(dp, shard, None), P(dp), P(dp + shard, None))
    out_specs = (P(dp + shard, None),) * 3
    return jax.shard_map(body, mesh=fine, in_specs=in_specs, out_specs=out_specs, check_vma=False)
```

```python
import functools

import jax
import jax.numpy as jnp
from jax import lax
from jax.experimental import pallas as pl
from jax.experimental.pallas import tpu as pltpu
from jax.sharding import Mesh, PartitionSpec as P

BLOCK = 128
AXES = ("ylo", "x", "yhi", "z", "core")
NZ = 16
FAR = NZ // 2
GROUPS = ((7, 6), (5, 4), (3, 2, 1, 0))
LATER = {6: (1, 0), 4: (2, 0), 3: (2, 2)}
CHAINS = ((0, 160), (160, 304), (304, 448))
VMEM = 56 * 1024 * 1024
f32 = jnp.float32
f16 = jnp.float16


def turn_kernel(len_ref, up_ref, feat_ref, *rest):
    outs, hold = list(rest[:-1]), rest[-1]
    step = pl.program_id(0)
    n_ex, seg, n_row = feat_ref.shape
    seg2, width = n_ex * seg, up_ref.shape[2] // 4
    span = width // NZ
    for half in range(2):
        turned = []
        for j in range(2):
            x = up_ref[:, :, (2 * j + half) * width:(2 * j + half + 1) * width]
            turned.append(x.reshape(seg2, width).astype(f32).T)
        for dest in range(NZ):
            rows = [t[dest * span:(dest + 1) * span] for t in turned]
            hold[half, dest, step] = jnp.concatenate(rows, axis=0).astype(hold.dtype)

    @pl.when(step == pl.num_programs(0) - 1)
    def _():
        n, tall = hold.shape[2], hold.shape[3]
        yhi, z, core = lax.axis_index("yhi"), lax.axis_index("z"), lax.axis_index("core")
        first_position = ((yhi * NZ + z) * 2 + core) * seg
        position = first_position + lax.broadcasted_iota(jnp.int32, (seg, n_row), 0)
        feats = jnp.concatenate([
            jnp.where(position < len_ref[e], feat_ref[e].astype(f32) * 0.25, 0.0) for e in range(n_ex)
        ], axis=0).astype(feat_ref.dtype)

        def put(out, at, half, to, dist, pairs):
            dest = lax.rem(z + (1 - 2 * to) * dist + NZ, NZ)
            for i, p in enumerate(pairs):
                out[at + i * tall:at + (i + 1) * tall] = hold[half, dest, p]
            return at + len(pairs) * tall

        def put_far(out, at, half, to):
            return put(out, at, half, to, FAR, [n // 2 * to + p for p in range(n // 2)])

        def put_features(out, at):
            for b in range(n_row // BLOCK):
                out[at + b * seg2:at + (b + 1) * seg2] = feats[:, b * BLOCK:(b + 1) * BLOCK]

        for i, half in enumerate((yhi, 1 - yhi)):
            n_out = 1 + len(GROUPS)
            first, *others = outs[n_out * i:n_out * (i + 1)]
            put_features(first, put_far(first, 0, half, core))
            for out, group in zip(others, GROUPS):
                at = 0
                for dist in group:
                    at = put(out, at, half, core, dist, range(n))
        first, other = outs[2 * n_out:]
        at = put_far(first, 0, yhi, 1 - core)
        put_features(first, put_far(first, at, 1 - yhi, 1 - core))
        at = 0
        for half in (yhi, 1 - yhi):
            for dist in sum(GROUPS, ()):
                at = put(other, at, half, 1 - core, dist, range(n))


def turn(upstream, features, lengths, n_groups):
    n_ex, seg, units = upstream.shape
    rows = features.shape[2]
    seg2 = n_ex * seg
    n = n_groups // 2
    chunk = units // 2 // NZ
    extra = rows // BLOCK * seg2
    heights = 2 * [chunk // 2 + extra, *(len(group) * chunk for group in GROUPS)]
    heights += [chunk + extra, 2 * FAR * chunk]
    whole = lambda shape: pl.BlockSpec(shape, lambda i, s: (0,) * len(shape))
    return pl.pallas_call(
        turn_kernel,
        grid_spec=pltpu.PrefetchScalarGridSpec(
            num_scalar_prefetch=1,
            grid=(n,),
            in_specs=[pl.BlockSpec((n_ex, seg, units // n), lambda i, s: (0, 0, i)), whole(features.shape)],
            out_specs=[whole((height, seg2)) for height in heights],
            scratch_shapes=[pltpu.VMEM((2, NZ, n, chunk // n, seg2), upstream.dtype)],
        ),
        out_shape=[jax.ShapeDtypeStruct((height, seg2), upstream.dtype) for height in heights],
        compiler_params=pltpu.CompilerParams(vmem_limit_bytes=VMEM),
    )(lengths, upstream, features)


def first_kernel(a_ref, b_ref, c_ref, d_ref, out_ref, right_ref):
    refs = (a_ref, b_ref, c_ref, d_ref)
    seg2 = a_ref.shape[1]
    height = out_ref.shape[0]
    n_lane = (a_ref.shape[0] - height) // seg2
    for k, ref in enumerate(refs):
        at = ref.shape[0] - n_lane * seg2
        rows = [ref[at + b * seg2:at + (b + 1) * seg2] for b in range(n_lane)]
        feats = jnp.concatenate(rows, axis=1)
        half = seg2 // 2
        none = jnp.zeros((half, feats.shape[1]), feats.dtype)
        right_ref[k * seg2:k * seg2 + half] = jnp.concatenate([feats[:half], none], axis=1)
        right_ref[k * seg2 + half:(k + 1) * seg2] = jnp.concatenate([none, feats[half:]], axis=1)
    left = jnp.concatenate([ref[:height] for ref in refs], axis=1)
    out_ref[...] = jnp.dot(left, right_ref[...], preferred_element_type=f32)


def first_product(pieces, height):
    seg2 = pieces[0].shape[1]
    wide = (pieces[0].shape[0] - height) // seg2 * BLOCK * 2
    return pl.pallas_call(
        first_kernel,
        out_shape=[
            jax.ShapeDtypeStruct((height, wide), f32),
            jax.ShapeDtypeStruct((4 * seg2, wide), pieces[0].dtype),
        ],
        cost_estimate=pl.CostEstimate(flops=200 * height * 4 * seg2 * wide, bytes_accessed=6 * height * wide, transcendentals=0),
        compiler_params=pltpu.CompilerParams(vmem_limit_bytes=40 * 1024 * 1024),
    )(*pieces)


def product_kernel(a_ref, b_ref, c_ref, d_ref, right_ref, out_ref):
    left = jnp.concatenate([ref[...] for ref in (a_ref, b_ref, c_ref, d_ref)], axis=1)
    out_ref[...] = jnp.dot(left, right_ref[...], preferred_element_type=f32)


def product(pieces, starts, right, chunk, count):
    seg2 = pieces[0].shape[1]
    tile = chunk // 2
    wide = right.shape[1]
    return pl.pallas_call(
        product_kernel,
        grid=(2 * count,),
        in_specs=[pl.BlockSpec((tile, seg2), lambda i, start=start: (2 * start + i, 0)) for start in starts]
        + [pl.BlockSpec(right.shape, lambda i: (0, 0))],
        out_specs=pl.BlockSpec((tile, wide), lambda i: (i, 0)),
        out_shape=jax.ShapeDtypeStruct((count * chunk, wide), f32),
        cost_estimate=pl.CostEstimate(
            flops=80 * count * chunk * 4 * seg2 * wide, bytes_accessed=6 * count * chunk * wide, transcendentals=0
        ),
        compiler_params=pltpu.CompilerParams(vmem_limit_bytes=40 * 1024 * 1024),
    )(*pieces, right)


def solve_kernel(shift, scale, g_ref, w_ref, inv_ref, sal_ref, step_ref, y_ref):
    n_ex = g_ref.shape[0]
    units = w_ref.shape[0]
    rows = w_ref.shape[1]
    pad = g_ref.shape[1]
    nb = rows // BLOCK

    def blocks(x):
        return jnp.concatenate([x[:, b * BLOCK:(b + 1) * BLOCK] for b in range(nb)], axis=0).T

    for e in range(n_ex):
        y_ref[e] = blocks(g_ref[e])
    weights = w_ref[...].astype(f32)
    w = blocks(jnp.concatenate([weights, jnp.zeros((pad - units, rows), f32)], axis=0))
    lane_rows = lax.broadcasted_iota(jnp.int32, (n_ex, BLOCK), 0)
    kern = []
    for i in range(n_ex):
        gi = y_ref[i]
        row = jnp.zeros((n_ex, BLOCK), f32)
        for j in range(i, n_ex):
            dot = jnp.sum(gi * y_ref[j], axis=0, keepdims=True)
            if j == i:
                dot = dot + shift
            row = jnp.where(lane_rows == j, dot, row)
        kern.append(row)
    diag = jnp.ones((BLOCK, BLOCK), f32)
    step = w
    for k in range(n_ex):
        pivot = kern[k]
        inv = 1.0 / pivot[k:k + 1]
        yk = y_ref[k]
        scaled = yk * inv
        diag = diag - yk * scaled
        step = step - scaled * jnp.sum(yk * w, axis=0, keepdims=True)
        for i in range(k + 1, n_ex):
            m = pivot[i:i + 1] * inv
            kern[i] = kern[i] - m * pivot
            y_ref[i] = y_ref[i] - m * yk
    diag = diag.T
    step = step.T * scale
    for b in range(nb):
        at = pl.ds(b * BLOCK, BLOCK)
        d = diag[b * pad:b * pad + units]
        wb = weights[:, b * BLOCK:(b + 1) * BLOCK]
        inv_ref[:, at] = d
        sal_ref[:, at] = rows * (wb * wb) / (2.0 * d)
        step_ref[:, at] = step[b * pad:b * pad + units]


def solve(grads, weights, shift):
    units, rows = weights.shape
    out = jax.ShapeDtypeStruct((units, rows), f32)
    return pl.pallas_call(
        functools.partial(solve_kernel, shift, float(rows) ** 0.5),
        out_shape=[out, out, out],
        scratch_shapes=[pltpu.VMEM((grads.shape[0], BLOCK, BLOCK), f32)],
        compiler_params=pltpu.CompilerParams(vmem_limit_bytes=40 * 1024 * 1024),
    )(grads, weights)


def ring_pairs(cross):
    pairs = []
    for z in range(NZ):
        for core in range(2):
            to = (z + 1 - 2 * core) % NZ
            pairs.append((z * 2 + core, to * 2 + (core ^ cross)))
    return pairs


def body(features, upstream, lengths, weights):
    core = lax.axis_index("core")
    _, seg, rows = features.shape
    units = upstream.shape[2]
    n_groups = 8
    total_len = seg * 64
    made = turn(upstream, features, lengths, n_groups)
    quad = lambda x, i: lax.ppermute(x, ("yhi", "core"), [(j, j ^ i) for j in range(4)])
    chunk = units // 2 // NZ
    half = chunk // 2
    n_out = 1 + len(GROUPS)
    after = lambda x, *events: lax.optimization_barrier((x, *events))[0]
    sizes = [len(group) * chunk for group in GROUPS]
    sib_far = quad(made[2 * n_out], 1)
    near = [quad(made[n_out], 2)]
    diag = [quad(sib_far[half:], 2)]
    far, right = first_product([made[0], sib_far, near[0], diag[0]], half)
    sib = quad(after(made[2 * n_out + 1], sib_far), 1)
    parts = {}

    def send(g, event):
        at = FAR * chunk + sum(sizes[:g])
        near.append(quad(after(made[n_out + 1 + g], event), 2))
        diag.append(quad(after(sib[at:at + sizes[g]], event), 2))

    def multiply(g, at, event):
        group = GROUPS[g]
        start = sum(map(len, GROUPS[:g])) + at
        pieces = [made[1 + g], sib, near[1 + g], after(diag[1 + g], event)]
        part = product(pieces, (at, start, at, at), right, chunk, 2)
        for i in range(2):
            parts[group[at + i]] = part[i * chunk:(i + 1) * chunk]
        return part

    ring = lambda x, cross=0: lax.ppermute(x, ("z", "core"), ring_pairs(cross))
    send(0, sib_far)
    send(1, far)
    nearest = multiply(0, 0, far)
    send(2, nearest)
    got, _ = lax.optimization_barrier((ring(far.astype(f16)), nearest))
    got = got.astype(f32)
    none = jnp.zeros_like(got)
    got = jnp.where(core == 0, jnp.concatenate([got, none], axis=0), jnp.concatenate([none, got], axis=0))
    sums = [(parts[FAR - 1][a:b] + got[a:b]).astype(f16) for a, b in CHAINS]
    last = sums[-1]
    for dist in range(FAR - 2, 0, -1):
        for k, (a, b) in enumerate(CHAINS):
            got = ring(sums[k])
            got = after(got, last)
            sums[k] = last = (got.astype(f32) + parts[dist][a:b]).astype(f16)
            if k == 0 and dist in LATER:
                multiply(*LATER[dist], last)
    pick = lambda x, i: lax.dynamic_slice_in_dim(x, i * rows, rows, 1)
    same = [ring(pick(x, core)).astype(f32) for x in sums]
    cross = ring(jnp.concatenate([pick(x, 1 - core) for x in sums], axis=0), 1).astype(f32)
    length = lax.dynamic_index_in_dim(lengths, core, 0, keepdims=False).astype(f32)
    total = (jnp.concatenate(same, axis=0) + cross + pick(parts[0], core)) * (4096.0 / length)
    pieces = total.astype(f16).reshape(2 * n_groups, -1, rows)
    owned = lax.all_to_all(pieces, ("ylo", "x", "core"), 0, 0, tiled=True)
    own_units = owned.shape[1]
    grads = owned.astype(f32) * (1.0 / 1024.0)
    grads = jnp.pad(grads, ((0, 0), (0, -own_units % 8), (0, 0)))
    return tuple(solve(grads, weights, BLOCK / total_len))


def solution(mesh):
    fine = Mesh(mesh.devices.reshape(2, 4, 2, NZ, 2), AXES)
    dp, shard = ("ylo", "x"), ("yhi", "z", "core")
    in_specs = (P(dp, shard, None), P(dp, shard, None), P(dp), P(dp + shard, None))
    out_specs = (P(dp + shard, None),) * 3
    return jax.shard_map(body, mesh=fine, in_specs=in_specs, out_specs=out_specs, check_vma=False)
```

```python
import functools

import jax
import jax.numpy as jnp
from jax import lax
from jax.experimental import pallas as pl
from jax.experimental.pallas import tpu as pltpu
from jax.sharding import Mesh, PartitionSpec as P

BLOCK = 128
AXES = ("ylo", "x", "yhi", "z", "core")
NZ = 16
FAR = NZ // 2
GROUPS = ((7, 6), (5, 4), (3, 2, 1, 0))
LATER = {6: (1, 0), 4: (2, 0), 3: (2, 2)}
DUE = {6: 1, 4: 2}
CHAINS = ((0, 160), (160, 304), (304, 448))
VMEM = 56 * 1024 * 1024
f32 = jnp.float32
f16 = jnp.float16


def turn_kernel(len_ref, up_ref, feat_ref, *rest):
    outs, hold = list(rest[:-1]), rest[-1]
    step = pl.program_id(0)
    n_ex, seg, n_row = feat_ref.shape
    seg2, width = n_ex * seg, up_ref.shape[2] // 4
    span = width // NZ
    for half in range(2):
        turned = []
        for j in range(2):
            x = up_ref[:, :, (2 * j + half) * width:(2 * j + half + 1) * width]
            turned.append(x.reshape(seg2, width).astype(f32).T)
        for dest in range(NZ):
            rows = [t[dest * span:(dest + 1) * span] for t in turned]
            hold[half, dest, step] = jnp.concatenate(rows, axis=0).astype(hold.dtype)

    @pl.when(step == pl.num_programs(0) - 1)
    def _():
        n, tall = hold.shape[2], hold.shape[3]
        yhi, z, core = lax.axis_index("yhi"), lax.axis_index("z"), lax.axis_index("core")
        first_position = ((yhi * NZ + z) * 2 + core) * seg
        position = first_position + lax.broadcasted_iota(jnp.int32, (seg, n_row), 0)
        feats = jnp.concatenate([
            jnp.where(position < len_ref[e], feat_ref[e].astype(f32) * 0.25, 0.0) for e in range(n_ex)
        ], axis=0).astype(feat_ref.dtype)

        def put(out, at, half, to, dist, pairs):
            dest = lax.rem(z + (1 - 2 * to) * dist + NZ, NZ)
            for i, p in enumerate(pairs):
                out[at + i * tall:at + (i + 1) * tall] = hold[half, dest, p]
            return at + len(pairs) * tall

        def put_far(out, at, half, to):
            return put(out, at, half, to, FAR, [n // 2 * to + p for p in range(n // 2)])

        def put_features(out, at):
            for b in range(n_row // BLOCK):
                out[at + b * seg2:at + (b + 1) * seg2] = feats[:, b * BLOCK:(b + 1) * BLOCK]

        for i, half in enumerate((yhi, 1 - yhi)):
            n_out = 1 + len(GROUPS)
            first, *others = outs[n_out * i:n_out * (i + 1)]
            put_features(first, put_far(first, 0, half, core))
            for out, group in zip(others, GROUPS):
                at = 0
                for dist in group:
                    at = put(out, at, half, core, dist, range(n))
        first, other = outs[2 * n_out:]
        at = put_far(first, 0, yhi, 1 - core)
        for half in (1 - yhi, yhi):
            for dist in GROUPS[0]:
                at = put(first, at, half, 1 - core, dist, range(n))
        put_features(first, put_far(first, at, 1 - yhi, 1 - core))
        at = 0
        for half in (yhi, 1 - yhi):
            for dist in sum(GROUPS[1:], ()):
                at = put(other, at, half, 1 - core, dist, range(n))


def turn(upstream, features, lengths, n_groups):
    n_ex, seg, units = upstream.shape
    rows = features.shape[2]
    seg2 = n_ex * seg
    n = n_groups // 2
    chunk = units // 2 // NZ
    extra = rows // BLOCK * seg2
    heights = 2 * [chunk // 2 + extra, *(len(group) * chunk for group in GROUPS)]
    heights += [chunk + 2 * len(GROUPS[0]) * chunk + extra, 2 * (FAR - len(GROUPS[0])) * chunk]
    whole = lambda shape: pl.BlockSpec(shape, lambda i, s: (0,) * len(shape))
    return pl.pallas_call(
        turn_kernel,
        grid_spec=pltpu.PrefetchScalarGridSpec(
            num_scalar_prefetch=1,
            grid=(n,),
            in_specs=[pl.BlockSpec((n_ex, seg, units // n), lambda i, s: (0, 0, i)), whole(features.shape)],
            out_specs=[whole((height, seg2)) for height in heights],
            scratch_shapes=[pltpu.VMEM((2, NZ, n, chunk // n, seg2), upstream.dtype)],
        ),
        out_shape=[jax.ShapeDtypeStruct((height, seg2), upstream.dtype) for height in heights],
        compiler_params=pltpu.CompilerParams(vmem_limit_bytes=VMEM),
    )(lengths, upstream, features)


def first_kernel(a_ref, b_ref, c_ref, d_ref, out_ref, right_ref):
    refs = (a_ref, b_ref, c_ref, d_ref)
    seg2 = a_ref.shape[1]
    height = out_ref.shape[0]
    n_lane = (a_ref.shape[0] - height) // seg2
    for k, ref in enumerate(refs):
        at = ref.shape[0] - n_lane * seg2
        rows = [ref[at + b * seg2:at + (b + 1) * seg2] for b in range(n_lane)]
        feats = jnp.concatenate(rows, axis=1)
        half = seg2 // 2
        none = jnp.zeros((half, feats.shape[1]), feats.dtype)
        right_ref[k * seg2:k * seg2 + half] = jnp.concatenate([feats[:half], none], axis=1)
        right_ref[k * seg2 + half:(k + 1) * seg2] = jnp.concatenate([none, feats[half:]], axis=1)
    left = jnp.concatenate([ref[:height] for ref in refs], axis=1)
    out_ref[...] = jnp.dot(left, right_ref[...], preferred_element_type=f32)


def first_product(pieces, height):
    seg2 = pieces[0].shape[1]
    wide = (pieces[0].shape[0] - height) // seg2 * BLOCK * 2
    return pl.pallas_call(
        first_kernel,
        out_shape=[
            jax.ShapeDtypeStruct((height, wide), f32),
            jax.ShapeDtypeStruct((4 * seg2, wide), pieces[0].dtype),
        ],
        cost_estimate=pl.CostEstimate(flops=200 * height * 4 * seg2 * wide, bytes_accessed=6 * height * wide, transcendentals=0),
        compiler_params=pltpu.CompilerParams(vmem_limit_bytes=12 * 1024 * 1024),
    )(*pieces)


def product_kernel(a_ref, b_ref, c_ref, d_ref, right_ref, out_ref):
    left = jnp.concatenate([ref[...] for ref in (a_ref, b_ref, c_ref, d_ref)], axis=1)
    out_ref[...] = jnp.dot(left, right_ref[...], preferred_element_type=f32)


def product(pieces, starts, right, chunk, count):
    seg2 = pieces[0].shape[1]
    tile = chunk // 2
    wide = right.shape[1]
    return pl.pallas_call(
        product_kernel,
        grid=(2 * count,),
        in_specs=[pl.BlockSpec((tile, seg2), lambda i, start=start: (start + i, 0)) for start in starts]
        + [pl.BlockSpec(right.shape, lambda i: (0, 0))],
        out_specs=pl.BlockSpec((tile, wide), lambda i: (i, 0)),
        out_shape=jax.ShapeDtypeStruct((count * chunk, wide), f32),
        cost_estimate=pl.CostEstimate(
            flops=80 * count * chunk * 4 * seg2 * wide, bytes_accessed=6 * count * chunk * wide, transcendentals=0
        ),
        compiler_params=pltpu.CompilerParams(vmem_limit_bytes=12 * 1024 * 1024),
    )(*pieces, right)


def solve_kernel(shift, scale, g_ref, w_ref, inv_ref, sal_ref, step_ref, y_ref):
    n_ex = g_ref.shape[0]
    units = w_ref.shape[0]
    rows = w_ref.shape[1]
    pad = g_ref.shape[1]
    nb = rows // BLOCK

    def blocks(x):
        return jnp.concatenate([x[:, b * BLOCK:(b + 1) * BLOCK] for b in range(nb)], axis=0).T

    for e in range(n_ex):
        y_ref[e] = blocks(g_ref[e])
    weights = w_ref[...].astype(f32)
    w = blocks(jnp.concatenate([weights, jnp.zeros((pad - units, rows), f32)], axis=0))
    lane_rows = lax.broadcasted_iota(jnp.int32, (n_ex, BLOCK), 0)
    kern = []
    for i in range(n_ex):
        gi = y_ref[i]
        row = jnp.zeros((n_ex, BLOCK), f32)
        for j in range(i, n_ex):
            dot = jnp.sum(gi * y_ref[j], axis=0, keepdims=True)
            if j == i:
                dot = dot + shift
            row = jnp.where(lane_rows == j, dot, row)
        kern.append(row)
    diag = jnp.ones((BLOCK, BLOCK), f32)
    step = w
    for k in range(n_ex):
        pivot = kern[k]
        inv = 1.0 / pivot[k:k + 1]
        yk = y_ref[k]
        scaled = yk * inv
        diag = diag - yk * scaled
        step = step - scaled * jnp.sum(yk * w, axis=0, keepdims=True)
        for i in range(k + 1, n_ex):
            m = pivot[i:i + 1] * inv
            kern[i] = kern[i] - m * pivot
            y_ref[i] = y_ref[i] - m * yk
    diag = diag.T
    step = step.T * scale
    for b in range(nb):
        at = pl.ds(b * BLOCK, BLOCK)
        d = diag[b * pad:b * pad + units]
        wb = weights[:, b * BLOCK:(b + 1) * BLOCK]
        inv_ref[:, at] = d
        sal_ref[:, at] = rows * (wb * wb) / (2.0 * d)
        step_ref[:, at] = step[b * pad:b * pad + units]


def solve(grads, weights, shift):
    units, rows = weights.shape
    out = jax.ShapeDtypeStruct((units, rows), f32)
    return pl.pallas_call(
        functools.partial(solve_kernel, shift, float(rows) ** 0.5),
        out_shape=[out, out, out],
        scratch_shapes=[pltpu.VMEM((grads.shape[0], BLOCK, BLOCK), f32)],
        compiler_params=pltpu.CompilerParams(vmem_limit_bytes=40 * 1024 * 1024),
    )(grads, weights)


def ring_pairs(cross):
    pairs = []
    for z in range(NZ):
        for core in range(2):
            to = (z + 1 - 2 * core) % NZ
            pairs.append((z * 2 + core, to * 2 + (core ^ cross)))
    return pairs


def body(features, upstream, lengths, weights):
    core = lax.axis_index("core")
    _, seg, rows = features.shape
    units = upstream.shape[2]
    n_groups = 8
    total_len = seg * 64
    made = turn(upstream, features, lengths, n_groups)
    quad = lambda x, i: lax.ppermute(x, ("yhi", "core"), [(j, j ^ i) for j in range(4)])
    chunk = units // 2 // NZ
    half = chunk // 2
    n_out = 1 + len(GROUPS)
    after = lambda x, *events: lax.optimization_barrier((x, *events))[0]
    sizes = [len(group) * chunk for group in GROUPS]
    sib_first = quad(made[2 * n_out], 1)
    far_at = sib_first.shape[0] - made[0].shape[0]
    far, right = first_product([made[0], sib_first, quad(made[n_out], 2), quad(sib_first[far_at:], 2)], half)
    sib_rest = quad(after(made[2 * n_out + 1], far), 1)

    def send(g, *events):
        at = half if g == 0 else sum(sizes[1:]) + sum(sizes[1:g])
        forward = (sib_first if g == 0 else sib_rest)[at:at + sizes[g]]
        both = after(jnp.concatenate([made[n_out + 1 + g], forward], axis=0), *events)
        sent.append(both)
        return quad(both, 2)

    parts, sent = {}, []

    def multiply(g, at, event):
        group = GROUPS[g]
        sib, sib_at = (sib_first, 1 + 2 * len(group)) if g == 0 else (sib_rest, 2 * sum(map(len, GROUPS[1:g])))
        away = after(arrived[g], event)
        starts = (2 * at, sib_at + 2 * at, 2 * at, 2 * len(group) + 2 * at)
        part = product([made[1 + g], sib, away, away], starts, right, chunk, 2)
        for i in range(2):
            parts[group[at + i]] = part[i * chunk:(i + 1) * chunk]
        return part

    ring = lambda x, cross=0: lax.ppermute(x, ("z", "core"), ring_pairs(cross))
    arrived = [send(0), send(1)]
    nearest = multiply(0, 0, far)
    arrived.append(send(2, far))
    got = after(ring(far.astype(f16)), nearest, *sent[1:])
    got = got.astype(f32)
    none = jnp.zeros_like(got)
    got = jnp.where(core == 0, jnp.concatenate([got, none], axis=0), jnp.concatenate([none, got], axis=0))
    sums = [(parts[FAR - 1][a:b] + got[a:b]).astype(f16) for a, b in CHAINS]
    last = sums[-1]
    for dist in range(FAR - 2, 0, -1):
        for k, (a, b) in enumerate(CHAINS):
            got = ring(sums[k])
            due = [arrived[DUE[dist]]] if k == 0 and dist in DUE else []
            got = after(got, last, *due)
            sums[k] = last = (got.astype(f32) + parts[dist][a:b]).astype(f16)
            if k == 0 and dist in LATER:
                multiply(*LATER[dist], last)
    pick = lambda x, i: lax.dynamic_slice_in_dim(x, i * rows, rows, 1)
    same = [ring(pick(x, core)).astype(f32) for x in sums]
    cross = ring(jnp.concatenate([pick(x, 1 - core) for x in sums], axis=0), 1).astype(f32)
    length = lax.dynamic_index_in_dim(lengths, core, 0, keepdims=False).astype(f32)
    total = (jnp.concatenate(same, axis=0) + cross + pick(parts[0], core)) * (4096.0 / length)
    pieces = total.astype(f16).reshape(2 * n_groups, -1, rows)
    owned = lax.all_to_all(pieces, ("ylo", "x", "core"), 0, 0, tiled=True)
    own_units = owned.shape[1]
    grads = owned.astype(f32) * (1.0 / 1024.0)
    grads = jnp.pad(grads, ((0, 0), (0, -own_units % 8), (0, 0)))
    return tuple(solve(grads, weights, BLOCK / total_len))


def solution(mesh):
    fine = Mesh(mesh.devices.reshape(2, 4, 2, NZ, 2), AXES)
    dp, shard = ("ylo", "x"), ("yhi", "z", "core")
    in_specs = (P(dp, shard, None), P(dp, shard, None), P(dp), P(dp + shard, None))
    out_specs = (P(dp + shard, None),) * 3
    return jax.shard_map(body, mesh=fine, in_specs=in_specs, out_specs=out_specs, check_vma=False)
```

```python
import functools

import jax
import jax.numpy as jnp
from jax import lax
from jax.experimental import pallas as pl
from jax.experimental.pallas import tpu as pltpu
from jax.sharding import Mesh, PartitionSpec as P

BLOCK = 128
AXES = ("ylo", "x", "yhi", "z", "core")
NZ = 16
FAR = NZ // 2
GROUPS = ((7, 6), (5, 4), (3, 2, 1, 0))
LATER = {6: (1, 0), 4: (2, 0), 3: (2, 2)}
DUE = {(6, 0): 1, (4, 0): 2}
CHAINS = ((0, 224), (224, 448))
VMEM = 56 * 1024 * 1024
f32 = jnp.float32
f16 = jnp.float16


def turn_kernel(len_ref, up_ref, feat_ref, *rest):
    outs, hold = list(rest[:-1]), rest[-1]
    step = pl.program_id(0)
    n_ex, seg, n_row = feat_ref.shape
    seg2, width = n_ex * seg, up_ref.shape[2] // 4
    span = width // NZ
    for half in range(2):
        turned = []
        for j in range(2):
            x = up_ref[:, :, (2 * j + half) * width:(2 * j + half + 1) * width]
            turned.append(x.reshape(seg2, width).astype(f32).T)
        for dest in range(NZ):
            rows = [t[dest * span:(dest + 1) * span] for t in turned]
            hold[half, dest, step] = jnp.concatenate(rows, axis=0).astype(hold.dtype)

    @pl.when(step == pl.num_programs(0) - 1)
    def _():
        n, tall = hold.shape[2], hold.shape[3]
        yhi, z, core = lax.axis_index("yhi"), lax.axis_index("z"), lax.axis_index("core")
        first_position = ((yhi * NZ + z) * 2 + core) * seg
        position = first_position + lax.broadcasted_iota(jnp.int32, (seg, n_row), 0)
        feats = jnp.concatenate([
            jnp.where(position < len_ref[e], feat_ref[e].astype(f32) * 0.25, 0.0) for e in range(n_ex)
        ], axis=0).astype(feat_ref.dtype)

        def put(out, at, half, to, dist, pairs):
            dest = lax.rem(z + (1 - 2 * to) * dist + NZ, NZ)
            for i, p in enumerate(pairs):
                out[at + i * tall:at + (i + 1) * tall] = hold[half, dest, p]
            return at + len(pairs) * tall

        def put_far(out, at, half, to):
            return put(out, at, half, to, FAR, [n // 2 * to + p for p in range(n // 2)])

        def put_features(out, at):
            for b in range(n_row // BLOCK):
                out[at + b * seg2:at + (b + 1) * seg2] = feats[:, b * BLOCK:(b + 1) * BLOCK]

        for i, half in enumerate((yhi, 1 - yhi)):
            n_out = 1 + len(GROUPS)
            first, *others = outs[n_out * i:n_out * (i + 1)]
            put_features(first, put_far(first, 0, half, core))
            for out, group in zip(others, GROUPS):
                at = 0
                for dist in group:
                    at = put(out, at, half, core, dist, range(n))
        first, other = outs[2 * n_out:]
        at = put_far(first, 0, yhi, 1 - core)
        for half in (1 - yhi, yhi):
            for dist in GROUPS[0]:
                at = put(first, at, half, 1 - core, dist, range(n))
        put_features(first, put_far(first, at, 1 - yhi, 1 - core))
        at = 0
        for half in (yhi, 1 - yhi):
            for dist in sum(GROUPS[1:], ()):
                at = put(other, at, half, 1 - core, dist, range(n))


def turn(upstream, features, lengths, n_groups):
    n_ex, seg, units = upstream.shape
    rows = features.shape[2]
    seg2 = n_ex * seg
    n = n_groups // 2
    chunk = units // 2 // NZ
    extra = rows // BLOCK * seg2
    heights = 2 * [chunk // 2 + extra, *(len(group) * chunk for group in GROUPS)]
    heights += [chunk + 2 * len(GROUPS[0]) * chunk + extra, 2 * (FAR - len(GROUPS[0])) * chunk]
    whole = lambda shape: pl.BlockSpec(shape, lambda i, s: (0,) * len(shape))
    return pl.pallas_call(
        turn_kernel,
        grid_spec=pltpu.PrefetchScalarGridSpec(
            num_scalar_prefetch=1,
            grid=(n,),
            in_specs=[pl.BlockSpec((n_ex, seg, units // n), lambda i, s: (0, 0, i)), whole(features.shape)],
            out_specs=[whole((height, seg2)) for height in heights],
            scratch_shapes=[pltpu.VMEM((2, NZ, n, chunk // n, seg2), upstream.dtype)],
        ),
        out_shape=[jax.ShapeDtypeStruct((height, seg2), upstream.dtype) for height in heights],
        compiler_params=pltpu.CompilerParams(vmem_limit_bytes=VMEM),
    )(lengths, upstream, features)


def first_kernel(a_ref, b_ref, c_ref, d_ref, out_ref, right_ref):
    refs = (a_ref, b_ref, c_ref, d_ref)
    seg2 = a_ref.shape[1]
    height = out_ref.shape[0]
    n_lane = (a_ref.shape[0] - height) // seg2
    for k, ref in enumerate(refs):
        at = ref.shape[0] - n_lane * seg2
        rows = [ref[at + b * seg2:at + (b + 1) * seg2] for b in range(n_lane)]
        feats = jnp.concatenate(rows, axis=1)
        half = seg2 // 2
        none = jnp.zeros((half, feats.shape[1]), feats.dtype)
        right_ref[k * seg2:k * seg2 + half] = jnp.concatenate([feats[:half], none], axis=1)
        right_ref[k * seg2 + half:(k + 1) * seg2] = jnp.concatenate([none, feats[half:]], axis=1)
    left = jnp.concatenate([ref[:height] for ref in refs], axis=1)
    out_ref[...] = jnp.dot(left, right_ref[...], preferred_element_type=f32)


def first_product(pieces, height):
    seg2 = pieces[0].shape[1]
    wide = (pieces[0].shape[0] - height) // seg2 * BLOCK * 2
    return pl.pallas_call(
        first_kernel,
        out_shape=[
            jax.ShapeDtypeStruct((height, wide), f32),
            jax.ShapeDtypeStruct((4 * seg2, wide), pieces[0].dtype),
        ],
        cost_estimate=pl.CostEstimate(flops=200 * height * 4 * seg2 * wide, bytes_accessed=6 * height * wide, transcendentals=0),
        compiler_params=pltpu.CompilerParams(vmem_limit_bytes=12 * 1024 * 1024),
    )(*pieces)


def product_kernel(a_ref, b_ref, c_ref, d_ref, right_ref, out_ref):
    left = jnp.concatenate([ref[...] for ref in (a_ref, b_ref, c_ref, d_ref)], axis=1)
    out_ref[...] = jnp.dot(left, right_ref[...], preferred_element_type=f32)


def product(pieces, starts, right, chunk, count):
    seg2 = pieces[0].shape[1]
    tile = chunk // 2
    wide = right.shape[1]
    return pl.pallas_call(
        product_kernel,
        grid=(2 * count,),
        in_specs=[pl.BlockSpec((tile, seg2), lambda i, start=start: (start + i, 0)) for start in starts]
        + [pl.BlockSpec(right.shape, lambda i: (0, 0))],
        out_specs=pl.BlockSpec((tile, wide), lambda i: (i, 0)),
        out_shape=jax.ShapeDtypeStruct((count * chunk, wide), f32),
        cost_estimate=pl.CostEstimate(
            flops=80 * count * chunk * 4 * seg2 * wide, bytes_accessed=6 * count * chunk * wide, transcendentals=0
        ),
        compiler_params=pltpu.CompilerParams(vmem_limit_bytes=12 * 1024 * 1024),
    )(*pieces, right)


def solve_kernel(shift, scale, g_ref, w_ref, inv_ref, sal_ref, step_ref, y_ref):
    n_ex = g_ref.shape[0]
    units = w_ref.shape[0]
    rows = w_ref.shape[1]
    pad = g_ref.shape[1]
    nb = rows // BLOCK

    def blocks(x):
        return jnp.concatenate([x[:, b * BLOCK:(b + 1) * BLOCK] for b in range(nb)], axis=0).T

    for e in range(n_ex):
        y_ref[e] = blocks(g_ref[e])
    weights = w_ref[...].astype(f32)
    w = blocks(jnp.concatenate([weights, jnp.zeros((pad - units, rows), f32)], axis=0))
    lane_rows = lax.broadcasted_iota(jnp.int32, (n_ex, BLOCK), 0)
    kern = []
    for i in range(n_ex):
        gi = y_ref[i]
        row = jnp.zeros((n_ex, BLOCK), f32)
        for j in range(i, n_ex):
            dot = jnp.sum(gi * y_ref[j], axis=0, keepdims=True)
            if j == i:
                dot = dot + shift
            row = jnp.where(lane_rows == j, dot, row)
        kern.append(row)
    diag = jnp.ones((BLOCK, BLOCK), f32)
    step = w
    for k in range(n_ex):
        pivot = kern[k]
        inv = 1.0 / pivot[k:k + 1]
        yk = y_ref[k]
        scaled = yk * inv
        diag = diag - yk * scaled
        step = step - scaled * jnp.sum(yk * w, axis=0, keepdims=True)
        for i in range(k + 1, n_ex):
            m = pivot[i:i + 1] * inv
            kern[i] = kern[i] - m * pivot
            y_ref[i] = y_ref[i] - m * yk
    diag = diag.T
    step = step.T * scale
    for b in range(nb):
        at = pl.ds(b * BLOCK, BLOCK)
        d = diag[b * pad:b * pad + units]
        wb = weights[:, b * BLOCK:(b + 1) * BLOCK]
        inv_ref[:, at] = d
        sal_ref[:, at] = rows * (wb * wb) / (2.0 * d)
        step_ref[:, at] = step[b * pad:b * pad + units]


def solve(grads, weights, shift):
    units, rows = weights.shape
    out = jax.ShapeDtypeStruct((units, rows), f32)
    return pl.pallas_call(
        functools.partial(solve_kernel, shift, float(rows) ** 0.5),
        out_shape=[out, out, out],
        scratch_shapes=[pltpu.VMEM((grads.shape[0], BLOCK, BLOCK), f32)],
        compiler_params=pltpu.CompilerParams(vmem_limit_bytes=12 * 1024 * 1024),
    )(grads, weights)


def ring_pairs(cross):
    pairs = []
    for z in range(NZ):
        for core in range(2):
            to = (z + 1 - 2 * core) % NZ
            pairs.append((z * 2 + core, to * 2 + (core ^ cross)))
    return pairs


def body(features, upstream, lengths, weights):
    core = lax.axis_index("core")
    _, seg, rows = features.shape
    units = upstream.shape[2]
    n_groups = 8
    total_len = seg * 64
    made = turn(upstream, features, lengths, n_groups)
    quad = lambda x, i: lax.ppermute(x, ("yhi", "core"), [(j, j ^ i) for j in range(4)])
    chunk = units // 2 // NZ
    half = chunk // 2
    n_out = 1 + len(GROUPS)
    after = lambda x, *events: lax.optimization_barrier((x, *events))[0]
    sizes = [len(group) * chunk for group in GROUPS]
    sib_first = quad(made[2 * n_out], 1)
    far_at = sib_first.shape[0] - made[0].shape[0]
    far, right = first_product([made[0], sib_first, quad(made[n_out], 2), quad(sib_first[far_at:], 2)], half)

    def send(g, *events):
        at = half if g == 0 else sum(sizes[1:]) + sum(sizes[1:g])
        forward = (sib_first if g == 0 else sib_rest)[at:at + sizes[g]]
        both = after(jnp.concatenate([made[n_out + 1 + g], forward], axis=0), *events)
        sent.append(both)
        return quad(both, 2)

    parts, sent = {}, []

    def multiply(g, at, event):
        group = GROUPS[g]
        sib, sib_at = (sib_first, 1 + 2 * len(group)) if g == 0 else (sib_rest, 2 * sum(map(len, GROUPS[1:g])))
        away = after(arrived[g], event)
        starts = (2 * at, sib_at + 2 * at, 2 * at, 2 * len(group) + 2 * at)
        part = product([made[1 + g], sib, away, away], starts, right, chunk, 2)
        for i in range(2):
            parts[group[at + i]] = part[i * chunk:(i + 1) * chunk]
        return part

    ring = lambda x, cross=0: lax.ppermute(x, ("z", "core"), ring_pairs(cross))
    arrived = [send(0)]
    sib_rest = quad(after(made[2 * n_out + 1], far), 1)
    arrived.append(send(1))
    nearest = multiply(0, 0, far)
    arrived.append(send(2, far))
    got = after(ring(far.astype(f16)), nearest, sent[1])
    got = got.astype(f32)
    none = jnp.zeros_like(got)
    got = jnp.where(core == 0, jnp.concatenate([got, none], axis=0), jnp.concatenate([none, got], axis=0))
    sums = [(parts[FAR - 1][a:b] + got[a:b]).astype(f16) for a, b in CHAINS]
    last = sums[-1]
    for dist in range(FAR - 2, 0, -1):
        for k, (a, b) in enumerate(CHAINS):
            got = ring(sums[k])
            due = [arrived[DUE[dist, k]]] if (dist, k) in DUE else []
            got = after(got, last, *due)
            sums[k] = last = (got.astype(f32) + parts[dist][a:b]).astype(f16)
            if k == 0 and dist in LATER:
                multiply(*LATER[dist], last)
    pick = lambda x, i: lax.dynamic_slice_in_dim(x, i * rows, rows, 1)
    same = [ring(pick(x, core)).astype(f32) for x in sums]
    cross = ring(jnp.concatenate([pick(x, 1 - core) for x in sums], axis=0), 1).astype(f32)
    length = lax.dynamic_index_in_dim(lengths, core, 0, keepdims=False).astype(f32)
    total = (jnp.concatenate(same, axis=0) + cross + pick(parts[0], core)) * (4096.0 / length)
    pieces = total.astype(f16).reshape(2 * n_groups, -1, rows)
    owned = lax.all_to_all(pieces, ("ylo", "x", "core"), 0, 0, tiled=True)
    own_units = owned.shape[1]
    grads = owned.astype(f32) * (1.0 / 1024.0)
    grads = jnp.pad(grads, ((0, 0), (0, -own_units % 8), (0, 0)))
    return tuple(solve(grads, weights, BLOCK / total_len))


def solution(mesh):
    fine = Mesh(mesh.devices.reshape(2, 4, 2, NZ, 2), AXES)
    dp, shard = ("ylo", "x"), ("yhi", "z", "core")
    in_specs = (P(dp, shard, None), P(dp, shard, None), P(dp), P(dp + shard, None))
    out_specs = (P(dp + shard, None),) * 3
    return jax.shard_map(body, mesh=fine, in_specs=in_specs, out_specs=out_specs, check_vma=False)
```

```python
import functools

import jax
import jax.numpy as jnp
from jax import lax
from jax.experimental import pallas as pl
from jax.experimental.pallas import tpu as pltpu
from jax.sharding import Mesh, PartitionSpec as P

BLOCK = 128
AXES = ("ylo", "x", "yhi", "z", "core")
NZ = 16
FAR = NZ // 2
GROUPS = ((7, 6), (5, 4), (3, 2, 1, 0))
LATER = {6: (1, 0), 4: (2, 0), 3: (2, 2)}
DUE = {(6, 1): 1, (4, 0): 2}
CHAINS = ((0, 224), (224, 448))
VMEM = 56 * 1024 * 1024
f32 = jnp.float32
f16 = jnp.float16


def turn_kernel(len_ref, up_ref, feat_ref, *rest):
    outs, hold = list(rest[:-1]), rest[-1]
    step = pl.program_id(0)
    n_ex, seg, n_row = feat_ref.shape
    seg2, width = n_ex * seg, up_ref.shape[2] // 4
    span = width // NZ
    for half in range(2):
        turned = []
        for j in range(2):
            x = up_ref[:, :, (2 * j + half) * width:(2 * j + half + 1) * width]
            turned.append(x.reshape(seg2, width).astype(f32).T)
        for dest in range(NZ):
            rows = [t[dest * span:(dest + 1) * span] for t in turned]
            hold[half, dest, step] = jnp.concatenate(rows, axis=0).astype(hold.dtype)

    @pl.when(step == pl.num_programs(0) - 1)
    def _():
        n, tall = hold.shape[2], hold.shape[3]
        yhi, z, core = lax.axis_index("yhi"), lax.axis_index("z"), lax.axis_index("core")
        first_position = ((yhi * NZ + z) * 2 + core) * seg
        position = first_position + lax.broadcasted_iota(jnp.int32, (seg, n_row), 0)
        feats = jnp.concatenate([
            jnp.where(position < len_ref[e], feat_ref[e].astype(f32) * 0.25, 0.0) for e in range(n_ex)
        ], axis=0).astype(feat_ref.dtype)

        def put(out, at, half, to, dist, pairs):
            dest = lax.rem(z + (1 - 2 * to) * dist + NZ, NZ)
            for i, p in enumerate(pairs):
                out[at + i * tall:at + (i + 1) * tall] = hold[half, dest, p]
            return at + len(pairs) * tall

        def put_far(out, at, half, to):
            return put(out, at, half, to, FAR, [n // 2 * to + p for p in range(n // 2)])

        def put_features(out, at):
            for b in range(n_row // BLOCK):
                out[at + b * seg2:at + (b + 1) * seg2] = feats[:, b * BLOCK:(b + 1) * BLOCK]

        for i, half in enumerate((yhi, 1 - yhi)):
            n_out = 1 + len(GROUPS)
            first, *others = outs[n_out * i:n_out * (i + 1)]
            put_features(first, put_far(first, 0, half, core))
            for out, group in zip(others, GROUPS):
                at = 0
                for dist in group:
                    at = put(out, at, half, core, dist, range(n))
        first, other = outs[2 * n_out:]
        at = put_far(first, 0, yhi, 1 - core)
        for half in (1 - yhi, yhi):
            for dist in GROUPS[0]:
                at = put(first, at, half, 1 - core, dist, range(n))
        put_features(first, put_far(first, at, 1 - yhi, 1 - core))
        at = 0
        for half in (yhi, 1 - yhi):
            for dist in sum(GROUPS[1:], ()):
                at = put(other, at, half, 1 - core, dist, range(n))


def turn(upstream, features, lengths, n_groups):
    n_ex, seg, units = upstream.shape
    rows = features.shape[2]
    seg2 = n_ex * seg
    n = n_groups // 2
    chunk = units // 2 // NZ
    extra = rows // BLOCK * seg2
    heights = 2 * [chunk // 2 + extra, *(len(group) * chunk for group in GROUPS)]
    heights += [chunk + 2 * len(GROUPS[0]) * chunk + extra, 2 * (FAR - len(GROUPS[0])) * chunk]
    whole = lambda shape: pl.BlockSpec(shape, lambda i, s: (0,) * len(shape))
    return pl.pallas_call(
        turn_kernel,
        grid_spec=pltpu.PrefetchScalarGridSpec(
            num_scalar_prefetch=1,
            grid=(n,),
            in_specs=[pl.BlockSpec((n_ex, seg, units // n), lambda i, s: (0, 0, i)), whole(features.shape)],
            out_specs=[whole((height, seg2)) for height in heights],
            scratch_shapes=[pltpu.VMEM((2, NZ, n, chunk // n, seg2), upstream.dtype)],
        ),
        out_shape=[jax.ShapeDtypeStruct((height, seg2), upstream.dtype) for height in heights],
        compiler_params=pltpu.CompilerParams(vmem_limit_bytes=VMEM),
    )(lengths, upstream, features)


def first_kernel(a_ref, b_ref, c_ref, d_ref, out_ref, right_ref):
    refs = (a_ref, b_ref, c_ref, d_ref)
    seg2 = a_ref.shape[1]
    height = out_ref.shape[0]
    n_lane = (a_ref.shape[0] - height) // seg2
    for k, ref in enumerate(refs):
        at = ref.shape[0] - n_lane * seg2
        rows = [ref[at + b * seg2:at + (b + 1) * seg2] for b in range(n_lane)]
        feats = jnp.concatenate(rows, axis=1)
        half = seg2 // 2
        none = jnp.zeros((half, feats.shape[1]), feats.dtype)
        right_ref[k * seg2:k * seg2 + half] = jnp.concatenate([feats[:half], none], axis=1)
        right_ref[k * seg2 + half:(k + 1) * seg2] = jnp.concatenate([none, feats[half:]], axis=1)
    left = jnp.concatenate([ref[:height] for ref in refs], axis=1)
    out_ref[...] = jnp.dot(left, right_ref[...], preferred_element_type=f32)


def first_product(pieces, height):
    seg2 = pieces[0].shape[1]
    wide = (pieces[0].shape[0] - height) // seg2 * BLOCK * 2
    return pl.pallas_call(
        first_kernel,
        out_shape=[
            jax.ShapeDtypeStruct((height, wide), f32),
            jax.ShapeDtypeStruct((4 * seg2, wide), pieces[0].dtype),
        ],
        cost_estimate=pl.CostEstimate(flops=200 * height * 4 * seg2 * wide, bytes_accessed=6 * height * wide, transcendentals=0),
        compiler_params=pltpu.CompilerParams(vmem_limit_bytes=12 * 1024 * 1024),
    )(*pieces)


def product_kernel(a_ref, b_ref, c_ref, d_ref, right_ref, out_ref):
    left = jnp.concatenate([ref[...] for ref in (a_ref, b_ref, c_ref, d_ref)], axis=1)
    out_ref[...] = jnp.dot(left, right_ref[...], preferred_element_type=f32)


def product(pieces, starts, right, chunk, count):
    seg2 = pieces[0].shape[1]
    tile = chunk // 2
    wide = right.shape[1]
    return pl.pallas_call(
        product_kernel,
        grid=(2 * count,),
        in_specs=[pl.BlockSpec((tile, seg2), lambda i, start=start: (start + i, 0)) for start in starts]
        + [pl.BlockSpec(right.shape, lambda i: (0, 0))],
        out_specs=pl.BlockSpec((tile, wide), lambda i: (i, 0)),
        out_shape=jax.ShapeDtypeStruct((count * chunk, wide), f32),
        cost_estimate=pl.CostEstimate(
            flops=80 * count * chunk * 4 * seg2 * wide, bytes_accessed=6 * count * chunk * wide, transcendentals=0
        ),
        compiler_params=pltpu.CompilerParams(vmem_limit_bytes=12 * 1024 * 1024),
    )(*pieces, right)


def solve_kernel(shift, scale, g_ref, w_ref, inv_ref, sal_ref, step_ref, y_ref):
    n_ex = g_ref.shape[0]
    units = w_ref.shape[0]
    rows = w_ref.shape[1]
    pad = g_ref.shape[1]
    nb = rows // BLOCK

    def blocks(x):
        return jnp.concatenate([x[:, b * BLOCK:(b + 1) * BLOCK] for b in range(nb)], axis=0).T

    for e in range(n_ex):
        y_ref[e] = blocks(g_ref[e])
    weights = w_ref[...].astype(f32)
    w = blocks(jnp.concatenate([weights, jnp.zeros((pad - units, rows), f32)], axis=0))
    lane_rows = lax.broadcasted_iota(jnp.int32, (n_ex, BLOCK), 0)
    kern = []
    for i in range(n_ex):
        gi = y_ref[i]
        row = jnp.zeros((n_ex, BLOCK), f32)
        for j in range(i, n_ex):
            dot = jnp.sum(gi * y_ref[j], axis=0, keepdims=True)
            if j == i:
                dot = dot + shift
            row = jnp.where(lane_rows == j, dot, row)
        kern.append(row)
    diag = jnp.ones((BLOCK, BLOCK), f32)
    step = w
    for k in range(n_ex):
        pivot = kern[k]
        inv = 1.0 / pivot[k:k + 1]
        yk = y_ref[k]
        scaled = yk * inv
        diag = diag - yk * scaled
        step = step - scaled * jnp.sum(yk * w, axis=0, keepdims=True)
        for i in range(k + 1, n_ex):
            m = pivot[i:i + 1] * inv
            kern[i] = kern[i] - m * pivot
            y_ref[i] = y_ref[i] - m * yk
    diag = diag.T
    step = step.T * scale
    for b in range(nb):
        at = pl.ds(b * BLOCK, BLOCK)
        d = diag[b * pad:b * pad + units]
        wb = weights[:, b * BLOCK:(b + 1) * BLOCK]
        inv_ref[:, at] = d
        sal_ref[:, at] = rows * (wb * wb) / (2.0 * d)
        step_ref[:, at] = step[b * pad:b * pad + units]


def solve(grads, weights, shift):
    units, rows = weights.shape
    out = jax.ShapeDtypeStruct((units, rows), f32)
    return pl.pallas_call(
        functools.partial(solve_kernel, shift, float(rows) ** 0.5),
        out_shape=[out, out, out],
        scratch_shapes=[pltpu.VMEM((grads.shape[0], BLOCK, BLOCK), f32)],
        compiler_params=pltpu.CompilerParams(vmem_limit_bytes=12 * 1024 * 1024),
    )(grads, weights)


def ring_pairs(cross):
    pairs = []
    for z in range(NZ):
        for core in range(2):
            to = (z + 1 - 2 * core) % NZ
            pairs.append((z * 2 + core, to * 2 + (core ^ cross)))
    return pairs


def body(features, upstream, lengths, weights):
    core = lax.axis_index("core")
    _, seg, rows = features.shape
    units = upstream.shape[2]
    n_groups = 8
    total_len = seg * 64
    made = turn(upstream, features, lengths, n_groups)
    quad = lambda x, i: lax.ppermute(x, ("yhi", "core"), [(j, j ^ i) for j in range(4)])
    chunk = units // 2 // NZ
    half = chunk // 2
    n_out = 1 + len(GROUPS)
    after = lambda x, *events: lax.optimization_barrier((x, *events))[0]
    sizes = [len(group) * chunk for group in GROUPS]
    sib_first = quad(made[2 * n_out], 1)
    far_at = sib_first.shape[0] - made[0].shape[0]
    far, right = first_product([made[0], sib_first, quad(made[n_out], 2), quad(sib_first[far_at:], 2)], half)

    def send(g, *events):
        at = half if g == 0 else sum(sizes[1:]) + sum(sizes[1:g])
        forward = (sib_first if g == 0 else sib_rest)[at:at + sizes[g]]
        both = after(jnp.concatenate([made[n_out + 1 + g], forward], axis=0), *events)
        sent.append(both)
        return quad(both, 2)

    parts, sent = {}, []

    def multiply(g, at, event):
        group = GROUPS[g]
        sib, sib_at = (sib_first, 1 + 2 * len(group)) if g == 0 else (sib_rest, 2 * sum(map(len, GROUPS[1:g])))
        away = after(arrived[g], event)
        starts = (2 * at, sib_at + 2 * at, 2 * at, 2 * len(group) + 2 * at)
        part = product([made[1 + g], sib, away, away], starts, right, chunk, 2)
        for i in range(2):
            parts[group[at + i]] = part[i * chunk:(i + 1) * chunk]
        return part

    ring = lambda x, cross=0: lax.ppermute(x, ("z", "core"), ring_pairs(cross))
    arrived = [send(0)]
    nearest = multiply(0, 0, far)
    quarter = half // 2
    got = [ring(far[i * quarter:(i + 1) * quarter].astype(f16)) for i in range(2)]
    sib_rest = quad(after(made[2 * n_out + 1], got[0]), 1)
    arrived += [send(1), send(2)]
    got = after(jnp.concatenate(got, axis=0), nearest)
    got = got.astype(f32)
    none = jnp.zeros_like(got)
    got = jnp.where(core == 0, jnp.concatenate([got, none], axis=0), jnp.concatenate([none, got], axis=0))
    sums = [(parts[FAR - 1][a:b] + got[a:b]).astype(f16) for a, b in CHAINS]
    last = sums[-1]
    for dist in range(FAR - 2, 0, -1):
        for k, (a, b) in enumerate(CHAINS):
            got = ring(sums[k])
            due = [arrived[DUE[dist, k]]] if (dist, k) in DUE else []
            if (dist, k) == (FAR - 2, 0):
                due.append(sent[1])
            got = after(got, last, *due)
            sums[k] = last = (got.astype(f32) + parts[dist][a:b]).astype(f16)
            if k == 0 and dist in LATER:
                multiply(*LATER[dist], last)
    pick = lambda x, i: lax.dynamic_slice_in_dim(x, i * rows, rows, 1)
    same = [ring(pick(x, core)).astype(f32) for x in sums]
    cross = ring(jnp.concatenate([pick(x, 1 - core) for x in sums], axis=0), 1).astype(f32)
    length = lax.dynamic_index_in_dim(lengths, core, 0, keepdims=False).astype(f32)
    total = (jnp.concatenate(same, axis=0) + cross + pick(parts[0], core)) * (4096.0 / length)
    pieces = total.astype(f16).reshape(2 * n_groups, -1, rows)
    owned = lax.all_to_all(pieces, ("ylo", "x", "core"), 0, 0, tiled=True)
    own_units = owned.shape[1]
    grads = owned.astype(f32) * (1.0 / 1024.0)
    grads = jnp.pad(grads, ((0, 0), (0, -own_units % 8), (0, 0)))
    return tuple(solve(grads, weights, BLOCK / total_len))


def solution(mesh):
    fine = Mesh(mesh.devices.reshape(2, 4, 2, NZ, 2), AXES)
    dp, shard = ("ylo", "x"), ("yhi", "z", "core")
    in_specs = (P(dp, shard, None), P(dp, shard, None), P(dp), P(dp + shard, None))
    out_specs = (P(dp + shard, None),) * 3
    return jax.shard_map(body, mesh=fine, in_specs=in_specs, out_specs=out_specs, check_vma=False)
```

```python
import functools

import jax
import jax.numpy as jnp
from jax import lax
from jax.experimental import pallas as pl
from jax.experimental.pallas import tpu as pltpu
from jax.sharding import Mesh, PartitionSpec as P

BLOCK = 128
AXES = ("ylo", "x", "yhi", "z", "core")
NZ = 16
FAR = NZ // 2
GROUPS = ((7, 6), (5, 4), (3, 2, 1, 0))
LATER = {6: (1, 0), 4: (2, 0), 3: (2, 2)}
DUE = {(6, 0): 1, (4, 0): 2}
VMEM = 56 * 1024 * 1024
f32 = jnp.float32
f16 = jnp.float16


def turn_kernel(len_ref, up_ref, feat_ref, *rest):
    outs, hold = list(rest[:-1]), rest[-1]
    step = pl.program_id(0)
    n_ex, seg, n_row = feat_ref.shape
    seg2, width = n_ex * seg, up_ref.shape[2] // 4
    span = width // NZ
    for half in range(2):
        turned = []
        for j in range(2):
            x = up_ref[:, :, (2 * j + half) * width:(2 * j + half + 1) * width]
            turned.append(x.reshape(seg2, width).astype(f32).T)
        for dest in range(NZ):
            rows = [t[dest * span:(dest + 1) * span] for t in turned]
            hold[half, dest, step] = jnp.concatenate(rows, axis=0).astype(hold.dtype)

    @pl.when(step == pl.num_programs(0) - 1)
    def _():
        n, tall = hold.shape[2], hold.shape[3]
        yhi, z, core = lax.axis_index("yhi"), lax.axis_index("z"), lax.axis_index("core")
        first_position = ((yhi * NZ + z) * 2 + core) * seg
        position = first_position + lax.broadcasted_iota(jnp.int32, (seg, n_row), 0)
        feats = jnp.concatenate([
            jnp.where(position < len_ref[e], feat_ref[e].astype(f32) * 0.25, 0.0) for e in range(n_ex)
        ], axis=0).astype(feat_ref.dtype)

        def put(out, at, half, to, dist, pairs):
            dest = lax.rem(z + (1 - 2 * to) * dist + NZ, NZ)
            for i, p in enumerate(pairs):
                out[at + i * tall:at + (i + 1) * tall] = hold[half, dest, p]
            return at + len(pairs) * tall

        def put_far(out, at, half, to):
            return put(out, at, half, to, FAR, [n // 2 * to + p for p in range(n // 2)])

        def put_features(out, at):
            for b in range(n_row // BLOCK):
                out[at + b * seg2:at + (b + 1) * seg2] = feats[:, b * BLOCK:(b + 1) * BLOCK]

        for i, half in enumerate((yhi, 1 - yhi)):
            n_out = 1 + len(GROUPS)
            first, *others = outs[n_out * i:n_out * (i + 1)]
            put_features(first, put_far(first, 0, half, core))
            for out, group in zip(others, GROUPS):
                at = 0
                for dist in group:
                    at = put(out, at, half, core, dist, range(n))
        first, other = outs[2 * n_out:]
        at = put_far(first, 0, yhi, 1 - core)
        for half in (1 - yhi, yhi):
            for dist in GROUPS[0]:
                at = put(first, at, half, 1 - core, dist, range(n))
        put_features(first, put_far(first, at, 1 - yhi, 1 - core))
        at = 0
        for half in (yhi, 1 - yhi):
            for dist in sum(GROUPS[1:], ()):
                at = put(other, at, half, 1 - core, dist, range(n))


def turn(upstream, features, lengths, n_groups):
    n_ex, seg, units = upstream.shape
    rows = features.shape[2]
    seg2 = n_ex * seg
    n = n_groups // 2
    chunk = units // 2 // NZ
    extra = rows // BLOCK * seg2
    heights = 2 * [chunk // 2 + extra, *(len(group) * chunk for group in GROUPS)]
    heights += [chunk + 2 * len(GROUPS[0]) * chunk + extra, 2 * (FAR - len(GROUPS[0])) * chunk]
    whole = lambda shape: pl.BlockSpec(shape, lambda i, s: (0,) * len(shape))
    return pl.pallas_call(
        turn_kernel,
        grid_spec=pltpu.PrefetchScalarGridSpec(
            num_scalar_prefetch=1,
            grid=(n,),
            in_specs=[pl.BlockSpec((n_ex, seg, units // n), lambda i, s: (0, 0, i)), whole(features.shape)],
            out_specs=[whole((height, seg2)) for height in heights],
            scratch_shapes=[pltpu.VMEM((2, NZ, n, chunk // n, seg2), upstream.dtype)],
        ),
        out_shape=[jax.ShapeDtypeStruct((height, seg2), upstream.dtype) for height in heights],
        compiler_params=pltpu.CompilerParams(vmem_limit_bytes=VMEM),
    )(lengths, upstream, features)


def first_kernel(a_ref, b_ref, c_ref, d_ref, out_ref, right_ref):
    own = lax.axis_index("core")
    refs = (a_ref, b_ref, c_ref, d_ref)
    seg2 = a_ref.shape[1]
    height = out_ref.shape[0]
    n_lane = (a_ref.shape[0] - height) // seg2
    for k, ref in enumerate(refs):
        at = ref.shape[0] - n_lane * seg2
        rows = [ref[at + b * seg2:at + (b + 1) * seg2] for b in range(n_lane)]
        feats = jnp.concatenate(rows, axis=1)
        half = seg2 // 2
        for e in range(2):
            mine = feats[e * half:(e + 1) * half].astype(f32)
            at = k * seg2 + e * half
            columns = [jnp.where(own == e, mine, 0.0), jnp.where(own == e, 0.0, mine)]
            right_ref[at:at + half] = jnp.concatenate(columns, axis=1).astype(feats.dtype)
    left = jnp.concatenate([ref[:height] for ref in refs], axis=1)
    out_ref[...] = jnp.dot(left, right_ref[...], preferred_element_type=f32)


def first_product(pieces, height):
    seg2 = pieces[0].shape[1]
    wide = (pieces[0].shape[0] - height) // seg2 * BLOCK * 2
    return pl.pallas_call(
        first_kernel,
        out_shape=[
            jax.ShapeDtypeStruct((height, wide), f32),
            jax.ShapeDtypeStruct((4 * seg2, wide), pieces[0].dtype),
        ],
        cost_estimate=pl.CostEstimate(flops=200 * height * 4 * seg2 * wide, bytes_accessed=6 * height * wide, transcendentals=0),
        compiler_params=pltpu.CompilerParams(vmem_limit_bytes=12 * 1024 * 1024),
    )(*pieces)


def product_kernel(a_ref, b_ref, c_ref, d_ref, right_ref, out_ref):
    left = jnp.concatenate([ref[...] for ref in (a_ref, b_ref, c_ref, d_ref)], axis=1)
    out_ref[...] = jnp.dot(left, right_ref[...], preferred_element_type=f32)


def product(pieces, starts, right, chunk, count):
    seg2 = pieces[0].shape[1]
    tile = chunk // 2
    wide = right.shape[1]
    return pl.pallas_call(
        product_kernel,
        grid=(2 * count,),
        in_specs=[pl.BlockSpec((tile, seg2), lambda i, start=start: (start + i, 0)) for start in starts]
        + [pl.BlockSpec(right.shape, lambda i: (0, 0))],
        out_specs=pl.BlockSpec((tile, wide), lambda i: (i, 0)),
        out_shape=jax.ShapeDtypeStruct((count * chunk, wide), f32),
        cost_estimate=pl.CostEstimate(
            flops=80 * count * chunk * 4 * seg2 * wide, bytes_accessed=6 * count * chunk * wide, transcendentals=0
        ),
        compiler_params=pltpu.CompilerParams(vmem_limit_bytes=12 * 1024 * 1024),
    )(*pieces, right)


def solve_kernel(shift, scale, g_ref, w_ref, inv_ref, sal_ref, step_ref, y_ref):
    n_ex = g_ref.shape[0]
    units = w_ref.shape[0]
    rows = w_ref.shape[1]
    pad = g_ref.shape[1]
    nb = rows // BLOCK

    def blocks(x):
        return jnp.concatenate([x[:, b * BLOCK:(b + 1) * BLOCK] for b in range(nb)], axis=0).T

    for e in range(n_ex):
        y_ref[e] = blocks(g_ref[e])
    weights = w_ref[...].astype(f32)
    w = blocks(jnp.concatenate([weights, jnp.zeros((pad - units, rows), f32)], axis=0))
    lane_rows = lax.broadcasted_iota(jnp.int32, (n_ex, BLOCK), 0)
    kern = []
    for i in range(n_ex):
        gi = y_ref[i]
        row = jnp.zeros((n_ex, BLOCK), f32)
        for j in range(i, n_ex):
            dot = jnp.sum(gi * y_ref[j], axis=0, keepdims=True)
            if j == i:
                dot = dot + shift
            row = jnp.where(lane_rows == j, dot, row)
        kern.append(row)
    diag = jnp.ones((BLOCK, BLOCK), f32)
    step = w
    for k in range(n_ex):
        pivot = kern[k]
        inv = 1.0 / pivot[k:k + 1]
        yk = y_ref[k]
        scaled = yk * inv
        diag = diag - yk * scaled
        step = step - scaled * jnp.sum(yk * w, axis=0, keepdims=True)
        for i in range(k + 1, n_ex):
            m = pivot[i:i + 1] * inv
            kern[i] = kern[i] - m * pivot
            y_ref[i] = y_ref[i] - m * yk
    diag = diag.T
    step = step.T * scale
    for b in range(nb):
        at = pl.ds(b * BLOCK, BLOCK)
        d = diag[b * pad:b * pad + units]
        wb = weights[:, b * BLOCK:(b + 1) * BLOCK]
        inv_ref[:, at] = d
        sal_ref[:, at] = rows * (wb * wb) / (2.0 * d)
        step_ref[:, at] = step[b * pad:b * pad + units]


def solve(grads, weights, shift):
    units, rows = weights.shape
    out = jax.ShapeDtypeStruct((units, rows), f32)
    return pl.pallas_call(
        functools.partial(solve_kernel, shift, float(rows) ** 0.5),
        out_shape=[out, out, out],
        scratch_shapes=[pltpu.VMEM((grads.shape[0], BLOCK, BLOCK), f32)],
        compiler_params=pltpu.CompilerParams(vmem_limit_bytes=12 * 1024 * 1024),
    )(grads, weights)


def ring_pairs(cross):
    pairs = []
    for z in range(NZ):
        for core in range(2):
            to = (z + 1 - 2 * core) % NZ
            pairs.append((z * 2 + core, to * 2 + (core ^ cross)))
    return pairs


def body(features, upstream, lengths, weights):
    core = lax.axis_index("core")
    _, seg, rows = features.shape
    units = upstream.shape[2]
    n_groups = 8
    total_len = seg * 64
    made = turn(upstream, features, lengths, n_groups)
    quad = lambda x, i: lax.ppermute(x, ("yhi", "core"), [(j, j ^ i) for j in range(4)])
    chunk = units // 2 // NZ
    half = chunk // 2
    n_out = 1 + len(GROUPS)
    after = lambda x, *events: lax.optimization_barrier((x, *events))[0]
    sizes = [len(group) * chunk for group in GROUPS]
    sib_first = quad(made[2 * n_out], 1)
    far_at = sib_first.shape[0] - made[0].shape[0]
    far, right = first_product([made[0], sib_first, quad(made[n_out], 2), quad(sib_first[far_at:], 2)], half)

    def send(g, *events):
        at = half if g == 0 else sum(sizes[1:]) + sum(sizes[1:g])
        forward = (sib_first if g == 0 else sib_rest)[at:at + sizes[g]]
        both = after(jnp.concatenate([made[n_out + 1 + g], forward], axis=0), *events)
        sent.append(both)
        return quad(both, 2)

    parts, sent = {}, []

    def multiply(g, at, event):
        group = GROUPS[g]
        sib, sib_at = (sib_first, 1 + 2 * len(group)) if g == 0 else (sib_rest, 2 * sum(map(len, GROUPS[1:g])))
        away = after(arrived[g], event)
        starts = (2 * at, sib_at + 2 * at, 2 * at, 2 * len(group) + 2 * at)
        part = product([made[1 + g], sib, away, away], starts, right, chunk, 2)
        for i in range(2):
            parts[group[at + i]] = part[i * chunk:(i + 1) * chunk]
        return part

    ring = lambda x, cross=0: lax.ppermute(x, ("z", "core"), ring_pairs(cross))
    arrived = [send(0)]
    sib_rest = quad(after(made[2 * n_out + 1], far), 1)
    arrived.append(send(1))
    nearest = multiply(0, 0, far)
    arrived.append(send(2, far))
    got = after(ring(far.astype(f16)), nearest, sent[1])
    got = got.astype(f32)
    none = jnp.zeros_like(got)
    got = jnp.where(core == 0, jnp.concatenate([got, none], axis=0), jnp.concatenate([none, got], axis=0))
    chains = ((0, rows), (rows, 2 * rows))
    sums = [(parts[FAR - 1][:, a:b] + got[:, a:b]).astype(f16) for a, b in chains]
    last = sums[-1]
    for dist in range(FAR - 2, 0, -1):
        for k, (a, b) in enumerate(chains):
            got = ring(sums[k])
            due = [arrived[DUE[dist, k]]] if (dist, k) in DUE else []
            got = after(got, last, *due)
            sums[k] = last = (got.astype(f32) + parts[dist][:, a:b]).astype(f16)
            if k == 0 and dist in LATER:
                multiply(*LATER[dist], last)
    total = after(ring(sums[0]), last).astype(f32) + parts[0][:, :rows]
    total = total + after(ring(sums[1], 1), total).astype(f32)
    length = lax.dynamic_index_in_dim(lengths, core, 0, keepdims=False).astype(f32)
    total = total * (4096.0 / length)
    pieces = total.astype(f16).reshape(2 * n_groups, -1, rows)
    owned = lax.all_to_all(pieces, ("ylo", "x", "core"), 0, 0, tiled=True)
    own_units = owned.shape[1]
    grads = owned.astype(f32) * (1.0 / 1024.0)
    grads = jnp.pad(grads, ((0, 0), (0, -own_units % 8), (0, 0)))
    return tuple(solve(grads, weights, BLOCK / total_len))


def solution(mesh):
    fine = Mesh(mesh.devices.reshape(2, 4, 2, NZ, 2), AXES)
    dp, shard = ("ylo", "x"), ("yhi", "z", "core")
    in_specs = (P(dp, shard, None), P(dp, shard, None), P(dp), P(dp + shard, None))
    out_specs = (P(dp + shard, None),) * 3
    return jax.shard_map(body, mesh=fine, in_specs=in_specs, out_specs=out_specs, check_vma=False)
```

```python
import functools

import jax
import jax.numpy as jnp
from jax import lax
from jax.experimental import pallas as pl
from jax.experimental.pallas import tpu as pltpu
from jax.sharding import Mesh, PartitionSpec as P

BLOCK = 128
AXES = ("ylo", "x", "yhi", "z", "core")
NZ = 16
FAR = NZ // 2
GROUPS = ((7, 6), (5, 4), (3, 2, 1, 0))
LATER = {6: (1, 0), 4: (2, 0), 2: (2, 2)}
DUE = {(6, 0): 1, (4, 0): 2}
VMEM = 56 * 1024 * 1024
f32 = jnp.float32
f16 = jnp.float16


def turn_kernel(len_ref, up_ref, feat_ref, *rest):
    outs, hold = list(rest[:-1]), rest[-1]
    step = pl.program_id(0)
    n_ex, seg, n_row = feat_ref.shape
    seg2, width = n_ex * seg, up_ref.shape[2] // 4
    span = width // NZ
    for half in range(2):
        turned = []
        for j in range(2):
            x = up_ref[:, :, (2 * j + half) * width:(2 * j + half + 1) * width]
            turned.append(x.reshape(seg2, width).astype(f32).T)
        for dest in range(NZ):
            rows = [t[dest * span:(dest + 1) * span] for t in turned]
            hold[half, dest, step] = jnp.concatenate(rows, axis=0).astype(hold.dtype)

    @pl.when(step == pl.num_programs(0) - 1)
    def _():
        n, tall = hold.shape[2], hold.shape[3]
        yhi, z, core = lax.axis_index("yhi"), lax.axis_index("z"), lax.axis_index("core")
        first_position = ((yhi * NZ + z) * 2 + core) * seg
        position = first_position + lax.broadcasted_iota(jnp.int32, (seg, n_row), 0)
        feats = jnp.concatenate([
            jnp.where(position < len_ref[e], feat_ref[e].astype(f32) * 0.25, 0.0) for e in range(n_ex)
        ], axis=0).astype(feat_ref.dtype)

        def put(out, at, half, to, dist, pairs):
            dest = lax.rem(z + (1 - 2 * to) * dist + NZ, NZ)
            for i, p in enumerate(pairs):
                out[at + i * tall:at + (i + 1) * tall] = hold[half, dest, p]
            return at + len(pairs) * tall

        def put_far(out, at, half, to):
            return put(out, at, half, to, FAR, [n // 2 * to + p for p in range(n // 2)])

        def put_features(out, at):
            for b in range(n_row // BLOCK):
                out[at + b * seg2:at + (b + 1) * seg2] = feats[:, b * BLOCK:(b + 1) * BLOCK]

        for i, half in enumerate((yhi, 1 - yhi)):
            n_out = 1 + len(GROUPS)
            first, *others = outs[n_out * i:n_out * (i + 1)]
            put_features(first, put_far(first, 0, half, core))
            for out, group in zip(others, GROUPS):
                at = 0
                for dist in group:
                    at = put(out, at, half, core, dist, range(n))
        first, other = outs[2 * n_out:]
        at = put_far(first, 0, yhi, 1 - core)
        for half in (1 - yhi, yhi):
            for dist in GROUPS[0]:
                at = put(first, at, half, 1 - core, dist, range(n))
        put_features(first, put_far(first, at, 1 - yhi, 1 - core))
        at = 0
        for half in (yhi, 1 - yhi):
            for dist in sum(GROUPS[1:], ()):
                at = put(other, at, half, 1 - core, dist, range(n))


def turn(upstream, features, lengths, n_groups):
    n_ex, seg, units = upstream.shape
    rows = features.shape[2]
    seg2 = n_ex * seg
    n = n_groups // 2
    chunk = units // 2 // NZ
    extra = rows // BLOCK * seg2
    heights = 2 * [chunk // 2 + extra, *(len(group) * chunk for group in GROUPS)]
    heights += [chunk + 2 * len(GROUPS[0]) * chunk + extra, 2 * (FAR - len(GROUPS[0])) * chunk]
    whole = lambda shape: pl.BlockSpec(shape, lambda i, s: (0,) * len(shape))
    return pl.pallas_call(
        turn_kernel,
        grid_spec=pltpu.PrefetchScalarGridSpec(
            num_scalar_prefetch=1,
            grid=(n,),
            in_specs=[pl.BlockSpec((n_ex, seg, units // n), lambda i, s: (0, 0, i)), whole(features.shape)],
            out_specs=[whole((height, seg2)) for height in heights],
            scratch_shapes=[pltpu.VMEM((2, NZ, n, chunk // n, seg2), upstream.dtype)],
        ),
        out_shape=[jax.ShapeDtypeStruct((height, seg2), upstream.dtype) for height in heights],
        compiler_params=pltpu.CompilerParams(vmem_limit_bytes=VMEM),
    )(lengths, upstream, features)


def first_kernel(a_ref, b_ref, c_ref, d_ref, out_ref, right_ref):
    own = lax.axis_index("core")
    refs = (a_ref, b_ref, c_ref, d_ref)
    seg2 = a_ref.shape[1]
    height = out_ref.shape[0]
    n_lane = (a_ref.shape[0] - height) // seg2
    for k, ref in enumerate(refs):
        at = ref.shape[0] - n_lane * seg2
        rows = [ref[at + b * seg2:at + (b + 1) * seg2] for b in range(n_lane)]
        feats = jnp.concatenate(rows, axis=1)
        half = seg2 // 2
        for e in range(2):
            mine = feats[e * half:(e + 1) * half].astype(f32)
            at = k * seg2 + e * half
            columns = [jnp.where(own == e, mine, 0.0), jnp.where(own == e, 0.0, mine)]
            right_ref[at:at + half] = jnp.concatenate(columns, axis=1).astype(feats.dtype)
    left = jnp.concatenate([ref[:height] for ref in refs], axis=1)
    out_ref[...] = jnp.dot(left, right_ref[...], preferred_element_type=f32)


def first_product(pieces, height):
    seg2 = pieces[0].shape[1]
    wide = (pieces[0].shape[0] - height) // seg2 * BLOCK * 2
    return pl.pallas_call(
        first_kernel,
        out_shape=[
            jax.ShapeDtypeStruct((height, wide), f32),
            jax.ShapeDtypeStruct((4 * seg2, wide), pieces[0].dtype),
        ],
        cost_estimate=pl.CostEstimate(flops=200 * height * 4 * seg2 * wide, bytes_accessed=6 * height * wide, transcendentals=0),
        compiler_params=pltpu.CompilerParams(vmem_limit_bytes=12 * 1024 * 1024),
    )(*pieces)


def product_kernel(a_ref, b_ref, c_ref, d_ref, right_ref, out_ref):
    left = jnp.concatenate([ref[...] for ref in (a_ref, b_ref, c_ref, d_ref)], axis=1)
    out_ref[...] = jnp.dot(left, right_ref[...], preferred_element_type=f32)


def product(pieces, starts, right, chunk, count):
    seg2 = pieces[0].shape[1]
    tile = chunk // 2
    wide = right.shape[1]
    return pl.pallas_call(
        product_kernel,
        grid=(2 * count,),
        in_specs=[pl.BlockSpec((tile, seg2), lambda i, start=start: (start + i, 0)) for start in starts]
        + [pl.BlockSpec(right.shape, lambda i: (0, 0))],
        out_specs=pl.BlockSpec((tile, wide), lambda i: (i, 0)),
        out_shape=jax.ShapeDtypeStruct((count * chunk, wide), f32),
        cost_estimate=pl.CostEstimate(
            flops=80 * count * chunk * 4 * seg2 * wide, bytes_accessed=6 * count * chunk * wide, transcendentals=0
        ),
        compiler_params=pltpu.CompilerParams(vmem_limit_bytes=12 * 1024 * 1024),
    )(*pieces, right)


def solve_kernel(shift, scale, g_ref, w_ref, inv_ref, sal_ref, step_ref, y_ref):
    n_ex = g_ref.shape[0]
    units = w_ref.shape[0]
    rows = w_ref.shape[1]
    pad = g_ref.shape[1]
    nb = rows // BLOCK

    def blocks(x):
        return jnp.concatenate([x[:, b * BLOCK:(b + 1) * BLOCK] for b in range(nb)], axis=0).T

    for e in range(n_ex):
        y_ref[e] = blocks(g_ref[e])
    weights = w_ref[...].astype(f32)
    w = blocks(jnp.concatenate([weights, jnp.zeros((pad - units, rows), f32)], axis=0))
    lane_rows = lax.broadcasted_iota(jnp.int32, (n_ex, BLOCK), 0)
    kern = []
    for i in range(n_ex):
        gi = y_ref[i]
        row = jnp.zeros((n_ex, BLOCK), f32)
        for j in range(i, n_ex):
            dot = jnp.sum(gi * y_ref[j], axis=0, keepdims=True)
            if j == i:
                dot = dot + shift
            row = jnp.where(lane_rows == j, dot, row)
        kern.append(row)
    diag = jnp.ones((BLOCK, BLOCK), f32)
    step = w
    for k in range(n_ex):
        pivot = kern[k]
        inv = 1.0 / pivot[k:k + 1]
        yk = y_ref[k]
        scaled = yk * inv
        diag = diag - yk * scaled
        step = step - scaled * jnp.sum(yk * w, axis=0, keepdims=True)
        for i in range(k + 1, n_ex):
            m = pivot[i:i + 1] * inv
            kern[i] = kern[i] - m * pivot
            y_ref[i] = y_ref[i] - m * yk
    diag = diag.T
    step = step.T * scale
    for b in range(nb):
        at = pl.ds(b * BLOCK, BLOCK)
        d = diag[b * pad:b * pad + units]
        wb = weights[:, b * BLOCK:(b + 1) * BLOCK]
        inv_ref[:, at] = d
        sal_ref[:, at] = rows * (wb * wb) / (2.0 * d)
        step_ref[:, at] = step[b * pad:b * pad + units]


def solve(grads, weights, shift):
    units, rows = weights.shape
    out = jax.ShapeDtypeStruct((units, rows), f32)
    return pl.pallas_call(
        functools.partial(solve_kernel, shift, float(rows) ** 0.5),
        out_shape=[out, out, out],
        scratch_shapes=[pltpu.VMEM((grads.shape[0], BLOCK, BLOCK), f32)],
        compiler_params=pltpu.CompilerParams(vmem_limit_bytes=12 * 1024 * 1024),
    )(grads, weights)


def ring_pairs(cross):
    pairs = []
    for z in range(NZ):
        for core in range(2):
            to = (z + 1 - 2 * core) % NZ
            pairs.append((z * 2 + core, to * 2 + (core ^ cross)))
    return pairs


def body(features, upstream, lengths, weights):
    core = lax.axis_index("core")
    _, seg, rows = features.shape
    units = upstream.shape[2]
    n_groups = 8
    total_len = seg * 64
    made = turn(upstream, features, lengths, n_groups)
    quad = lambda x, i: lax.ppermute(x, ("yhi", "core"), [(j, j ^ i) for j in range(4)])
    chunk = units // 2 // NZ
    half = chunk // 2
    n_out = 1 + len(GROUPS)
    after = lambda x, *events: lax.optimization_barrier((x, *events))[0]
    sizes = [len(group) * chunk for group in GROUPS]
    sib_first = quad(made[2 * n_out], 1)
    far_at = sib_first.shape[0] - made[0].shape[0]
    far, right = first_product([made[0], sib_first, quad(made[n_out], 2), quad(sib_first[far_at:], 2)], half)

    def send(g, *events):
        at = half if g == 0 else sum(sizes[1:]) + sum(sizes[1:g])
        forward = (sib_first if g == 0 else sib_rest)[at:at + sizes[g]]
        both = after(jnp.concatenate([made[n_out + 1 + g], forward], axis=0), *events)
        sent.append(both)
        return quad(both, 2)

    parts, sent = {}, []

    def multiply(g, at, event):
        group = GROUPS[g]
        sib, sib_at = (sib_first, 1 + 2 * len(group)) if g == 0 else (sib_rest, 2 * sum(map(len, GROUPS[1:g])))
        away = after(arrived[g], event)
        starts = (2 * at, sib_at + 2 * at, 2 * at, 2 * len(group) + 2 * at)
        part = product([made[1 + g], sib, away, away], starts, right, chunk, 2)
        for i in range(2):
            parts[group[at + i]] = part[i * chunk:(i + 1) * chunk]
        return part

    ring = lambda x, cross=0: lax.ppermute(x, ("z", "core"), ring_pairs(cross))
    arrived = [send(0)]
    far16 = far.astype(f16)
    sib_rest = quad(after(made[2 * n_out + 1], far16), 1)
    arrived.append(send(1))
    nearest = multiply(0, 0, far)
    arrived.append(send(2, far))
    got = after(ring(far16), nearest, sent[1])
    got = got.astype(f32)
    none = jnp.zeros_like(got)
    got = jnp.where(core == 0, jnp.concatenate([got, none], axis=0), jnp.concatenate([none, got], axis=0))
    chains = ((0, rows), (rows, 2 * rows))
    sums = [(parts[FAR - 1][:, a:b] + got[:, a:b]).astype(f16) for a, b in chains]
    last = sums[-1]
    for dist in range(FAR - 2, 0, -1):
        for k, (a, b) in enumerate(chains):
            got = ring(sums[k])
            due = [arrived[DUE[dist, k]]] if (dist, k) in DUE else []
            got = after(got, last, *due)
            sums[k] = last = (got.astype(f32) + parts[dist][:, a:b]).astype(f16)
            if k == 0 and dist in LATER:
                multiply(*LATER[dist], last)
    total = after(ring(sums[0]), last).astype(f32) + parts[0][:, :rows]
    total = total + after(ring(sums[1], 1), total).astype(f32)
    length = lax.dynamic_index_in_dim(lengths, core, 0, keepdims=False).astype(f32)
    total = total * (4096.0 / length)
    pieces = total.astype(f16).reshape(2 * n_groups, -1, rows)
    owned = lax.all_to_all(pieces, ("ylo", "x", "core"), 0, 0, tiled=True)
    own_units = owned.shape[1]
    grads = owned.astype(f32) * (1.0 / 1024.0)
    grads = jnp.pad(grads, ((0, 0), (0, -own_units % 8), (0, 0)))
    return tuple(solve(grads, weights, BLOCK / total_len))


def solution(mesh):
    fine = Mesh(mesh.devices.reshape(2, 4, 2, NZ, 2), AXES)
    dp, shard = ("ylo", "x"), ("yhi", "z", "core")
    in_specs = (P(dp, shard, None), P(dp, shard, None), P(dp), P(dp + shard, None))
    out_specs = (P(dp + shard, None),) * 3
    return jax.shard_map(body, mesh=fine, in_specs=in_specs, out_specs=out_specs, check_vma=False)
```

```python
import functools

import jax
import jax.numpy as jnp
from jax import lax
from jax.experimental import pallas as pl
from jax.experimental.pallas import tpu as pltpu
from jax.sharding import Mesh, PartitionSpec as P

BLOCK = 128
AXES = ("ylo", "x", "yhi", "z", "core")
NZ = 16
FAR = NZ // 2
GROUPS = ((7, 6), (5, 4), (3, 2, 1, 0))
LATER = {6: (1, 0), 4: (2, 0), 2: (2, 2)}
DUE = {(6, 0): 1, (4, 0): 2}
VMEM = 56 * 1024 * 1024
f32 = jnp.float32
f16 = jnp.float16


def turn_kernel(len_ref, up_ref, feat_ref, *rest):
    outs, hold = list(rest[:-1]), rest[-1]
    step = pl.program_id(0)
    n_ex, seg, n_row = feat_ref.shape
    seg2, width = n_ex * seg, up_ref.shape[2] // 4
    span = width // NZ
    for half in range(2):
        turned = []
        for j in range(2):
            x = up_ref[:, :, (2 * j + half) * width:(2 * j + half + 1) * width]
            turned.append(x.reshape(seg2, width).astype(f32).T)
        for dest in range(NZ):
            rows = [t[dest * span:(dest + 1) * span] for t in turned]
            hold[half, dest, step] = jnp.concatenate(rows, axis=0).astype(hold.dtype)

    @pl.when(step == pl.num_programs(0) - 1)
    def _():
        n, tall = hold.shape[2], hold.shape[3]
        yhi, z, core = lax.axis_index("yhi"), lax.axis_index("z"), lax.axis_index("core")
        first_position = ((yhi * NZ + z) * 2 + core) * seg
        position = first_position + lax.broadcasted_iota(jnp.int32, (seg, n_row), 0)
        feats = jnp.concatenate([
            jnp.where(position < len_ref[e], feat_ref[e].astype(f32) * 0.25, 0.0) for e in range(n_ex)
        ], axis=0).astype(feat_ref.dtype)

        def put(out, at, half, to, dist, pairs):
            dest = lax.rem(z + (1 - 2 * to) * dist + NZ, NZ)
            for i, p in enumerate(pairs):
                out[at + i * tall:at + (i + 1) * tall] = hold[half, dest, p]
            return at + len(pairs) * tall

        def put_far(out, at, half, to):
            return put(out, at, half, to, FAR, [n // 2 * to + p for p in range(n // 2)])

        def put_features(out, at):
            for b in range(n_row // BLOCK):
                out[at + b * seg2:at + (b + 1) * seg2] = feats[:, b * BLOCK:(b + 1) * BLOCK]

        for i, half in enumerate((yhi, 1 - yhi)):
            n_out = 1 + len(GROUPS)
            first, *others = outs[n_out * i:n_out * (i + 1)]
            put_features(first, put_far(first, 0, half, core))
            for out, group in zip(others, GROUPS):
                at = 0
                for dist in group:
                    at = put(out, at, half, core, dist, range(n))
        first, other = outs[2 * n_out:]
        at = put_far(first, 0, yhi, 1 - core)
        for half in (1 - yhi, yhi):
            for dist in GROUPS[0]:
                at = put(first, at, half, 1 - core, dist, range(n))
        put_features(first, put_far(first, at, 1 - yhi, 1 - core))
        at = 0
        for half in (yhi, 1 - yhi):
            for dist in sum(GROUPS[1:], ()):
                at = put(other, at, half, 1 - core, dist, range(n))


def turn(upstream, features, lengths, n_groups):
    n_ex, seg, units = upstream.shape
    rows = features.shape[2]
    seg2 = n_ex * seg
    n = n_groups // 2
    chunk = units // 2 // NZ
    extra = rows // BLOCK * seg2
    heights = 2 * [chunk // 2 + extra, *(len(group) * chunk for group in GROUPS)]
    heights += [chunk + 2 * len(GROUPS[0]) * chunk + extra, 2 * (FAR - len(GROUPS[0])) * chunk]
    whole = lambda shape: pl.BlockSpec(shape, lambda i, s: (0,) * len(shape))
    return pl.pallas_call(
        turn_kernel,
        grid_spec=pltpu.PrefetchScalarGridSpec(
            num_scalar_prefetch=1,
            grid=(n,),
            in_specs=[pl.BlockSpec((n_ex, seg, units // n), lambda i, s: (0, 0, i)), whole(features.shape)],
            out_specs=[whole((height, seg2)) for height in heights],
            scratch_shapes=[pltpu.VMEM((2, NZ, n, chunk // n, seg2), upstream.dtype)],
        ),
        out_shape=[jax.ShapeDtypeStruct((height, seg2), upstream.dtype) for height in heights],
        compiler_params=pltpu.CompilerParams(vmem_limit_bytes=VMEM),
    )(lengths, upstream, features)


def first_kernel(a_ref, b_ref, c_ref, d_ref, out_ref, right_ref):
    own = lax.axis_index("core")
    refs = (a_ref, b_ref, c_ref, d_ref)
    seg2 = a_ref.shape[1]
    height = out_ref.shape[0]
    n_lane = (a_ref.shape[0] - height) // seg2
    for k, ref in enumerate(refs):
        at = ref.shape[0] - n_lane * seg2
        rows = [ref[at + b * seg2:at + (b + 1) * seg2] for b in range(n_lane)]
        feats = jnp.concatenate(rows, axis=1)
        half = seg2 // 2
        for e in range(2):
            mine = feats[e * half:(e + 1) * half].astype(f32)
            at = k * seg2 + e * half
            columns = [jnp.where(own == e, mine, 0.0), jnp.where(own == e, 0.0, mine)]
            right_ref[at:at + half] = jnp.concatenate(columns, axis=1).astype(feats.dtype)
    left = jnp.concatenate([ref[:height] for ref in refs], axis=1)
    out_ref[...] = jnp.dot(left, right_ref[...], preferred_element_type=f32)


def first_product(pieces, height):
    seg2 = pieces[0].shape[1]
    wide = (pieces[0].shape[0] - height) // seg2 * BLOCK * 2
    return pl.pallas_call(
        first_kernel,
        out_shape=[
            jax.ShapeDtypeStruct((height, wide), f32),
            jax.ShapeDtypeStruct((4 * seg2, wide), pieces[0].dtype),
        ],
        cost_estimate=pl.CostEstimate(flops=200 * height * 4 * seg2 * wide, bytes_accessed=6 * height * wide, transcendentals=0),
        compiler_params=pltpu.CompilerParams(vmem_limit_bytes=12 * 1024 * 1024),
    )(*pieces)


def product_kernel(a_ref, b_ref, c_ref, d_ref, right_ref, out_ref):
    left = jnp.concatenate([ref[...] for ref in (a_ref, b_ref, c_ref, d_ref)], axis=1)
    out_ref[...] = jnp.dot(left, right_ref[...], preferred_element_type=f32)


def product(pieces, starts, right, chunk, count):
    seg2 = pieces[0].shape[1]
    tile = chunk // 2
    wide = right.shape[1]
    return pl.pallas_call(
        product_kernel,
        grid=(2 * count,),
        in_specs=[pl.BlockSpec((tile, seg2), lambda i, start=start: (start + i, 0)) for start in starts]
        + [pl.BlockSpec(right.shape, lambda i: (0, 0))],
        out_specs=pl.BlockSpec((tile, wide), lambda i: (i, 0)),
        out_shape=jax.ShapeDtypeStruct((count * chunk, wide), f32),
        cost_estimate=pl.CostEstimate(
            flops=80 * count * chunk * 4 * seg2 * wide, bytes_accessed=6 * count * chunk * wide, transcendentals=0
        ),
        compiler_params=pltpu.CompilerParams(vmem_limit_bytes=12 * 1024 * 1024),
    )(*pieces, right)


def solve_kernel(shift, scale, g_ref, w_ref, inv_ref, sal_ref, step_ref, y_ref):
    n_ex = g_ref.shape[0]
    units = w_ref.shape[0]
    rows = w_ref.shape[1]
    pad = g_ref.shape[1]
    nb = rows // BLOCK

    def blocks(x):
        return jnp.concatenate([x[:, b * BLOCK:(b + 1) * BLOCK] for b in range(nb)], axis=0).T

    for e in range(n_ex):
        y_ref[e] = blocks(g_ref[e])
    weights = w_ref[...].astype(f32)
    w = blocks(jnp.concatenate([weights, jnp.zeros((pad - units, rows), f32)], axis=0))
    lane_rows = lax.broadcasted_iota(jnp.int32, (n_ex, BLOCK), 0)
    kern = []
    for i in range(n_ex):
        gi = y_ref[i]
        row = jnp.zeros((n_ex, BLOCK), f32)
        for j in range(i, n_ex):
            dot = jnp.sum(gi * y_ref[j], axis=0, keepdims=True)
            if j == i:
                dot = dot + shift
            row = jnp.where(lane_rows == j, dot, row)
        kern.append(row)
    diag = jnp.ones((BLOCK, BLOCK), f32)
    step = w
    for k in range(n_ex):
        pivot = kern[k]
        inv = 1.0 / pivot[k:k + 1]
        yk = y_ref[k]
        scaled = yk * inv
        diag = diag - yk * scaled
        step = step - scaled * jnp.sum(yk * w, axis=0, keepdims=True)
        for i in range(k + 1, n_ex):
            m = pivot[i:i + 1] * inv
            kern[i] = kern[i] - m * pivot
            y_ref[i] = y_ref[i] - m * yk
    diag = diag.T
    step = step.T * scale
    for b in range(nb):
        at = pl.ds(b * BLOCK, BLOCK)
        d = diag[b * pad:b * pad + units]
        wb = weights[:, b * BLOCK:(b + 1) * BLOCK]
        inv_ref[:, at] = d
        sal_ref[:, at] = rows * (wb * wb) / (2.0 * d)
        step_ref[:, at] = step[b * pad:b * pad + units]


def solve(grads, weights, shift):
    units, rows = weights.shape
    out = jax.ShapeDtypeStruct((units, rows), f32)
    return pl.pallas_call(
        functools.partial(solve_kernel, shift, float(rows) ** 0.5),
        out_shape=[out, out, out],
        scratch_shapes=[pltpu.VMEM((grads.shape[0], BLOCK, BLOCK), f32)],
        compiler_params=pltpu.CompilerParams(vmem_limit_bytes=12 * 1024 * 1024),
    )(grads, weights)


def ring_pairs(cross):
    pairs = []
    for z in range(NZ):
        for core in range(2):
            to = (z + 1 - 2 * core) % NZ
            pairs.append((z * 2 + core, to * 2 + (core ^ cross)))
    return pairs


def body(features, upstream, lengths, weights):
    core = lax.axis_index("core")
    _, seg, rows = features.shape
    units = upstream.shape[2]
    n_groups = 8
    total_len = seg * 64
    made = turn(upstream, features, lengths, n_groups)
    quad = lambda x, i: lax.ppermute(x, ("yhi", "core"), [(j, j ^ i) for j in range(4)])
    chunk = units // 2 // NZ
    half = chunk // 2
    n_out = 1 + len(GROUPS)
    after = lambda x, *events: lax.optimization_barrier((x, *events))[0]
    sizes = [len(group) * chunk for group in GROUPS]
    sib_first = quad(made[2 * n_out], 1)
    far_at = sib_first.shape[0] - made[0].shape[0]
    far, right = first_product([made[0], sib_first, quad(made[n_out], 2), quad(sib_first[far_at:], 2)], half)

    def send(g, *events):
        at = half if g == 0 else sum(sizes[1:]) + sum(sizes[1:g])
        forward = (sib_first if g == 0 else sib_rest)[at:at + sizes[g]]
        both = after(jnp.concatenate([made[n_out + 1 + g], forward], axis=0), *events)
        sent.append(both)
        return quad(both, 2)

    parts, sent = {}, []

    def multiply(g, at, event):
        group = GROUPS[g]
        sib, sib_at = (sib_first, 1 + 2 * len(group)) if g == 0 else (sib_rest, 2 * sum(map(len, GROUPS[1:g])))
        away = after(arrived[g], event)
        starts = (2 * at, sib_at + 2 * at, 2 * at, 2 * len(group) + 2 * at)
        part = product([made[1 + g], sib, away, away], starts, right, chunk, 2)
        for i in range(2):
            parts[group[at + i]] = part[i * chunk:(i + 1) * chunk]
        return part

    ring = lambda x, cross=0: lax.ppermute(x, ("z", "core"), ring_pairs(cross))
    far16 = far.astype(f16)
    arrived = [send(0, far16)]
    sib_rest = quad(after(made[2 * n_out + 1], far16), 1)
    arrived.append(send(1))
    nearest = multiply(0, 0, far)
    arrived.append(send(2, far))
    got = after(ring(far16), nearest, sent[1])
    got = got.astype(f32)
    none = jnp.zeros_like(got)
    got = jnp.where(core == 0, jnp.concatenate([got, none], axis=0), jnp.concatenate([none, got], axis=0))
    chains = ((0, rows), (rows, 2 * rows))
    sums = [(parts[FAR - 1][:, a:b] + got[:, a:b]).astype(f16) for a, b in chains]
    last = sums[-1]
    for dist in range(FAR - 2, 0, -1):
        for k, (a, b) in enumerate(chains):
            got = ring(sums[k])
            due = [arrived[DUE[dist, k]]] if (dist, k) in DUE else []
            got = after(got, last, *due)
            sums[k] = last = (got.astype(f32) + parts[dist][:, a:b]).astype(f16)
            if k == 0 and dist in LATER:
                multiply(*LATER[dist], last)
    total = after(ring(sums[0]), last).astype(f32) + parts[0][:, :rows]
    total = total + after(ring(sums[1], 1), total).astype(f32)
    length = lax.dynamic_index_in_dim(lengths, core, 0, keepdims=False).astype(f32)
    total = total * (4096.0 / length)
    pieces = total.astype(f16).reshape(2 * n_groups, -1, rows)
    owned = lax.all_to_all(pieces, ("ylo", "x", "core"), 0, 0, tiled=True)
    own_units = owned.shape[1]
    grads = owned.astype(f32) * (1.0 / 1024.0)
    grads = jnp.pad(grads, ((0, 0), (0, -own_units % 8), (0, 0)))
    return tuple(solve(grads, weights, BLOCK / total_len))


def solution(mesh):
    fine = Mesh(mesh.devices.reshape(2, 4, 2, NZ, 2), AXES)
    dp, shard = ("ylo", "x"), ("yhi", "z", "core")
    in_specs = (P(dp, shard, None), P(dp, shard, None), P(dp), P(dp + shard, None))
    out_specs = (P(dp + shard, None),) * 3
    return jax.shard_map(body, mesh=fine, in_specs=in_specs, out_specs=out_specs, check_vma=False)
```
